32 devices in a mesh: det: 2 (over core), grp: 4 (over y, x), filt: 4 (over z).
Axes of the slice: x: 2, y: 2, z: 4, core: 2. Of those that a mesh axis runs over, the one named last changes fastest.
Arguments:
- strain: float32 [2, 131072], P('det'), may hold values from -6 to 6
- inv_asd: float32 [2, 65536], P('det'), may hold values from 0.25 to 4
- templates: bfloat16 [192, 4096], P(('grp', 'filt')), may hold values from -6 to 6
- chirp_blocks: int32 [192], P(('grp', 'filt')), may hold values from 1 to 32, as said below
- owner: int32 [192], P(('grp', 'filt')), may hold values from 0 to 3, as said below
- slide: int32 [4], P('grp'), may hold values from 0 to 1023
Outputs:
- peaks: float32 [192, 1024], P(('grp', 'filt'), 'det')
- loudest: float32 [1024], P('det')
The draws below stay inside these ranges and needn't reach their ends.
Inputs may be any that keep to these rules, and one draw needn't show every extreme that they name: `chirp_blocks`: every device holds a template of 32 blocks. Each device sends either 3 or none of its templates to each owner of its group, and each owner receives exactly 12 templates.
All inputs are finite; a program needn't handle non-finite values.
Results may differ from the reference program's by a relative error of at most 0.0052.
Values may be sent and summed in bfloat16 or wider, within the bound.
No kernel may reach another device: no remote copies, remote signals or barrier semaphores. Data moves between devices by JAX's collectives and lax.ppermute only.
A program may use at most 64 MiB of HBM per device.

```python
import math
import jax
import jax.numpy as jnp
from jax import lax

N1 = 256
N2 = 512
NFFT = 131072
BLK = 128
MAXB = 32
TL = 4096
NBLK = 1024
TPL_DEV = 12
CAP = 3
TEMPLATES = 192
N_DET = 2
N_GRP = 4
N_FILT = 4


def draw_chirp_blocks(key, part):
    devices = N_GRP * N_FILT
    lengths = jax.random.randint(jax.random.fold_in(key, 21), (devices, TPL_DEV), 1, MAXB + 1)
    longest = jax.random.randint(jax.random.fold_in(key, 22), (devices, 1), 0, TPL_DEV)
    lengths = jnp.where(jnp.arange(TPL_DEV, dtype=jnp.int32)[None, :] == longest, MAXB, lengths)
    return lengths.reshape(TEMPLATES).astype(jnp.int32)


def draw_owner(key, part):
    shift_keys = jax.random.split(jax.random.fold_in(key, 11), N_GRP)
    shifts = jax.vmap(lambda shift_key: jax.random.permutation(shift_key, N_FILT)[:TPL_DEV // CAP])(shift_keys)
    source = jnp.arange(N_FILT, dtype=jnp.int32)[None, :, None]
    picked = jnp.arange(TPL_DEV, dtype=jnp.int32) // CAP
    based = (source + shifts[:, None, picked].astype(jnp.int32)) % N_FILT
    scores = jax.random.randint(jax.random.fold_in(key, 12), (N_GRP, N_FILT, TPL_DEV), 0, 1 << 20) * TPL_DEV
    scores = scores + jnp.arange(TPL_DEV, dtype=jnp.int32)
    shuffle = jnp.argsort(scores, axis=-1)
    return jnp.take_along_axis(based, shuffle, axis=-1).reshape(TEMPLATES).astype(jnp.int32)


def touch_ends(values, own_key, low, top_value):
    longest = values.shape.index(max(values.shape))
    spots = []
    for shift in (0, 1):
        where = [jax.random.randint(jax.random.fold_in(own_key, axis), (), 0, length) for axis, length in enumerate(values.shape)]
        where[longest] = (where[longest] + shift) % values.shape[longest]
        spots.append(tuple(where))
    return values.at[spots[0]].set(low).at[spots[1]].set(top_value)


def block_levels(rng, dims, cuts, smallest, top_value):
    loudness, own = 1.0, jax.random.fold_in(rng, 6)
    for position, parts in cuts:
        draws = jnp.exp(jax.random.uniform(jax.random.fold_in(own, position), (parts,), jnp.float32, smallest / len(cuts), top_value / len(cuts)))
        loudness = loudness * jnp.repeat(draws, dims[position] // parts).reshape([-1 if axis == position else 1 for axis in range(len(dims))])
    return loudness


def scatter_about(rng, extent, width, reach, cuts=(), kind=jnp.bfloat16):
    loudness = block_levels(rng, extent, cuts, -0.22, 0.18) if cuts else 1.0
    array = jax.random.normal(rng, extent, jnp.float32) * width * loudness
    return jnp.minimum(jnp.maximum(array, -reach), reach).astype(kind)


def setup_inputs(seed: int = 0) -> dict:
    arg_keys = jax.random.split(jax.random.key(seed), 7)
    return {
        "strain": scatter_about(arg_keys[0], (N_DET, NFFT), 1.0, 6.0, ((0, 2),), jnp.float32),
        "inv_asd": jnp.clip(jnp.exp(math.log(4.0) - 2.7725887 * jax.random.uniform(arg_keys[1], (N_DET, NFFT // 2), jnp.float32) ** block_levels(arg_keys[1], (N_DET, NFFT // 2), ((0, 2),), -0.2, 0.2)), 0.25, 4.0),
        "templates": scatter_about(arg_keys[2], (TEMPLATES, TL), 1.0, 6.0, ((0, 16),)),
        "chirp_blocks": draw_chirp_blocks(jax.random.fold_in(arg_keys[6], 71), 0),
        "owner": draw_owner(jax.random.fold_in(arg_keys[6], 71), 0),
        "slide": touch_ends(jax.random.randint(arg_keys[5], (N_GRP,), 0, NBLK), jax.random.fold_in(arg_keys[5], 1), 0, NBLK - 1).astype(jnp.int32),
    }


TWO_PI = 6.283185307179586


def angle_table(rows, cols, period):
    left = jnp.arange(rows, dtype=jnp.int32)[:, None]
    right = jnp.arange(cols, dtype=jnp.int32)[None, :]
    return (TWO_PI / period) * ((left * right) % period).astype(jnp.float32)


def make_tables():
    first = angle_table(N1, N1, N1)
    twist = angle_table(N1, N2, NFFT)
    second = angle_table(N2, N2 // 2, N2)
    back = angle_table(N2 // 2, N2, N2)
    return (jnp.cos(first).astype(jnp.bfloat16), jnp.sin(first).astype(jnp.bfloat16),
            jnp.cos(twist), jnp.sin(twist),
            jnp.cos(second).astype(jnp.bfloat16), jnp.sin(second).astype(jnp.bfloat16),
            jnp.cos(back).astype(jnp.bfloat16), jnp.sin(back).astype(jnp.bfloat16))


def forward(signal, cos_rows, sin_rows, tables):
    cos_first, sin_first, cos_twist, sin_twist, cos_second, sin_second, cos_back, sin_back = tables
    real_a = jnp.dot(cos_rows, signal, preferred_element_type=jnp.float32)
    imag_a = -jnp.dot(sin_rows, signal, preferred_element_type=jnp.float32)
    real_b = (real_a * cos_twist + imag_a * sin_twist).astype(jnp.bfloat16)
    imag_b = (imag_a * cos_twist - real_a * sin_twist).astype(jnp.bfloat16)
    real_x = jnp.dot(real_b, cos_second, preferred_element_type=jnp.float32) + jnp.dot(imag_b, sin_second, preferred_element_type=jnp.float32)
    imag_x = jnp.dot(imag_b, cos_second, preferred_element_type=jnp.float32) - jnp.dot(real_b, sin_second, preferred_element_type=jnp.float32)
    return real_x, imag_x


def correlate(windowed, spectrum, weight2d, tables):
    cos_first, sin_first, cos_twist, sin_twist, cos_second, sin_second, cos_back, sin_back = tables
    rows_used = windowed.shape[0]
    temp_real, temp_imag = forward(windowed, cos_first[:, :rows_used], sin_first[:, :rows_used], tables)
    sigma = jnp.sum(weight2d * weight2d * (temp_real * temp_real + temp_imag * temp_imag))
    data_real, data_imag = spectrum
    q_real = (temp_real * data_real + temp_imag * data_imag).astype(jnp.bfloat16)
    q_imag = (temp_real * data_imag - temp_imag * data_real).astype(jnp.bfloat16)
    d_real = jnp.dot(q_real, cos_back, preferred_element_type=jnp.float32) - jnp.dot(q_imag, sin_back, preferred_element_type=jnp.float32)
    d_imag = jnp.dot(q_real, sin_back, preferred_element_type=jnp.float32) + jnp.dot(q_imag, cos_back, preferred_element_type=jnp.float32)
    e_real = (d_real * cos_twist - d_imag * sin_twist).astype(jnp.bfloat16)
    e_imag = (d_real * sin_twist + d_imag * cos_twist).astype(jnp.bfloat16)
    z_real = jnp.dot(cos_first, e_real, preferred_element_type=jnp.float32) - jnp.dot(sin_first, e_imag, preferred_element_type=jnp.float32)
    z_imag = jnp.dot(sin_first, e_real, preferred_element_type=jnp.float32) + jnp.dot(cos_first, e_imag, preferred_element_type=jnp.float32)
    return ((z_real * z_real + z_imag * z_imag) / (NFFT * sigma)).reshape(NFFT)


def data_spectrum(strain_row, weight_row, tables):
    weight2d = weight_row.reshape(N2 // 2, N1).T
    signal = strain_row.astype(jnp.bfloat16).reshape(N1, N2)
    real_s, imag_s = forward(signal, tables[0], tables[1], tables)
    return (weight2d * real_s, weight2d * imag_s), weight2d


def reference(strain, inv_asd, templates, chirp_blocks, owner, slide):
    tables = make_tables()
    first_spec, first_weight = data_spectrum(strain[0], inv_asd[0], tables)
    second_spec, second_weight = data_spectrum(strain[1], inv_asd[1], tables)
    group_of = jnp.arange(TEMPLATES, dtype=jnp.int32) // (N_FILT * TPL_DEV)
    owner_order = jnp.argsort(group_of * N_FILT + owner, stable=True).astype(jnp.int32)
    samples = jnp.arange(TL, dtype=jnp.int32)

    def filter_template(template_id):
        bank_row = templates[template_id]
        windowed = jnp.where(samples < BLK * chirp_blocks[template_id], bank_row, jnp.zeros_like(bank_row))
        windowed = windowed.reshape(TL // N2, N2)
        first_snr = correlate(windowed, first_spec, first_weight, tables)
        second_snr = correlate(windowed, second_spec, second_weight, tables)
        slide_shift = BLK * slide[group_of[template_id]]
        network = first_snr + jnp.roll(second_snr, -slide_shift)
        return jnp.max(network.reshape(NBLK, BLK), axis=1)

    peaks = lax.map(filter_template, owner_order)
    loudest = jnp.max(peaks, axis=0)
    return peaks, loudest
```

```python
import functools

import jax
import jax.numpy as jnp
import ml_dtypes
import numpy as np
from jax import lax
from jax.experimental import pallas as pl
from jax.experimental.pallas import tpu as pltpu
from jax.sharding import PartitionSpec as P

N1 = 256
N2 = 512
NFFT = 131072
BLK = 128
NBLK = 1024
TL = 4096
ROWS = TL // N2
SLAB = 16
HALF = 128
BF16 = jnp.bfloat16
F32 = jnp.float32


def wave(left, right, period):
    angle = 2.0 * np.pi * ((np.asarray(left)[:, None] * np.asarray(right)[None, :]) % period) / period
    return np.cos(angle).astype(np.float32), np.sin(angle).astype(np.float32)


def make_tables():
    ar = np.arange
    cos_first, sin_first = wave(ar(N1), ar(N1), N1)
    first = np.concatenate([cos_first, -sin_first], axis=1)
    spread = np.repeat(first[:ROWS], SLAB, axis=0)
    cos_twist, sin_twist = wave(ar(N2), ar(N1), NFFT)
    ahead, back, last = [], [], []
    for parity in range(2):
        bins = 2 * ar(HALF) + parity
        cos_m, sin_m = wave(bins, ar(N1), N2)
        ahead.append(np.block([[cos_m, sin_m], [-sin_m, cos_m]]))
        back.append(np.block([[cos_m.T, -sin_m.T], [sin_m.T, cos_m.T]]))
        cos_l, sin_l = wave(ar(HALF), bins, N1)
        last.append(np.block([[cos_l, sin_l], [-sin_l, cos_l]]))
    low = lambda value: np.asarray(value, dtype=ml_dtypes.bfloat16)
    return dict(
        first=low(first),
        spread=low(spread),
        cos_twist=cos_twist,
        sin_twist=sin_twist,
        ahead=low(np.stack(ahead)),
        back=low(np.stack(back)),
        last=low(np.stack(last)),
    )


def dot(left, right):
    return jnp.dot(left, right, preferred_element_type=F32)


FWD_CHUNK = 64
INV_CHUNK = 64


def forward(signal, first, cos_t, sin_t, ahead, folded):
    for start in range(0, N1, FWD_CHUNK):
        parts = []
        for base in (start, start + N1):
            rows = pl.ds(base, FWD_CHUNK)
            both = dot(signal[rows, :], first)
            real_a, imag_a = both[:, :N1], both[:, N1:]
            cos_c, sin_c = cos_t[rows, :], sin_t[rows, :]
            parts.append((real_a * cos_c + imag_a * sin_c, imag_a * cos_c - real_a * sin_c))
        (real_l, imag_l), (real_u, imag_u) = parts
        folded[0, pl.ds(start, FWD_CHUNK), :] = (real_l + real_u).astype(BF16)
        folded[0, pl.ds(start + N1, FWD_CHUNK), :] = (imag_l + imag_u).astype(BF16)
        folded[1, pl.ds(start, FWD_CHUNK), :] = (real_l - real_u).astype(BF16)
        folded[1, pl.ds(start + N1, FWD_CHUNK), :] = (imag_l - imag_u).astype(BF16)
    return dot(ahead[0], folded[0]), dot(ahead[1], folded[1])


def data_spectrum(shift, strain, weight, first, cos_t, sin_t, ahead, twice, flipped, folded, spec, weight2d):
    twice[pl.ds(0, NBLK), :] = strain[...]
    twice[pl.ds(NBLK, NBLK), :] = strain[...]
    for part in range(N2 // BLK):
        block = twice[pl.ds(shift + part, N1, stride=N2 // BLK), :]
        flipped[pl.ds(part * BLK, BLK), :] = block.T.astype(BF16)
    halves = forward(flipped, first[...], cos_t, sin_t, ahead, folded)
    for parity in range(2):
        for part in range(2):
            weight2d[parity, :, pl.ds(part * HALF, HALF)] = weight[pl.ds(2 * parity + part, HALF, stride=4), :]
        kept = weight2d[parity]
        spec[parity, pl.ds(0, HALF), :] = halves[parity][:HALF] * kept
        spec[parity, pl.ds(HALF, HALF), :] = halves[parity][HALF:] * kept


def bank_kernel(scalars, blocks, templates, strain, weight, spread, first, cos_t, sin_t, ahead,
                bank, spec, weight2d, twice, flipped, folded, slabs, bank_t):
    step = pl.program_id(0)
    mine = pl.num_programs(0)
    total = templates.shape[0]

    @pl.when(step == 0)
    def _():
        slabs[...] = jnp.zeros_like(slabs)
        row = lax.broadcasted_iota(jnp.int32, (total, N2), 0)
        column = lax.broadcasted_iota(jnp.int32, (total, N2), 1)
        limit = jnp.zeros((total, N2), jnp.int32)
        for index in range(total):
            limit = jnp.where(row == index, BLK * blocks[index], limit)
        for part in range(ROWS):
            piece = templates[:, pl.ds(part * N2, N2)].astype(F32)
            slabs[pl.ds(part * SLAB, total), :] = jnp.where(column + part * N2 < limit, piece, 0.0)
        bank_t[...] = slabs[...].T.astype(BF16)
        data_spectrum(scalars[0], strain, weight, first, cos_t, sin_t, ahead, twice, flipped, folded, spec, weight2d)

    slot = lax.broadcasted_iota(jnp.int32, spread.shape, 0) % SLAB
    picked = jnp.where(slot == scalars[1] * mine + step, spread[...].astype(F32), 0.0).astype(BF16)
    even, odd = forward(bank_t, picked, cos_t, sin_t, ahead, folded)
    bank[0, 0] = even
    bank[0, 1] = odd


def filter_kernel(scalars, bank, spec_own, weight_own, strain, weight, first, cos_t, sin_t, ahead, back, last,
                  peaks, spec, weight2d, twice, flipped, folded, product, lines):
    @pl.when(pl.program_id(0) == 0)
    def _():
        data_spectrum(scalars[0], strain, weight, first, cos_t, sin_t, ahead, twice, flipped, folded, spec, weight2d)

    sigmas = []
    for side, (spectrum, weights) in enumerate(((spec_own, weight_own), (spec, weight2d))):
        sigma = jnp.zeros((1, 1), F32)
        for parity in range(2):
            bank_r, bank_i = bank[0, parity, :HALF], bank[0, parity, HALF:]
            data_r, data_i = spectrum[parity, :HALF], spectrum[parity, HALF:]
            kept = weights[parity]
            power = kept * kept * (bank_r * bank_r + bank_i * bank_i)
            sigma = sigma + jnp.sum(jnp.sum(power, axis=0, keepdims=True), axis=1, keepdims=True)
            product[parity, pl.ds(0, HALF), :] = (bank_r * data_r + bank_i * data_i).astype(BF16)
            product[parity, pl.ds(HALF, HALF), :] = (bank_r * data_i - bank_i * data_r).astype(BF16)
        sigmas.append(sigma)
        for start in range(0, N1, INV_CHUNK):
            low, high = pl.ds(start, INV_CHUNK), pl.ds(start + N1, INV_CHUNK)
            real_e, imag_e = dot(back[0, low, :], product[0]), dot(back[0, high, :], product[0])
            real_o, imag_o = dot(back[1, low, :], product[1]), dot(back[1, high, :], product[1])
            for rows, real_d, imag_d in ((low, real_e + real_o, imag_e + imag_o), (high, real_e - real_o, imag_e - imag_o)):
                cos_c, sin_c = cos_t[rows, :], sin_t[rows, :]
                real_w = real_d * cos_c - imag_d * sin_c
                imag_w = real_d * sin_c + imag_d * cos_c
                lines[side, 0, rows, :HALF] = (real_w[:, :HALF] + real_w[:, HALF:]).astype(BF16)
                lines[side, 0, rows, HALF:] = (imag_w[:, :HALF] + imag_w[:, HALF:]).astype(BF16)
                lines[side, 1, rows, :HALF] = (real_w[:, :HALF] - real_w[:, HALF:]).astype(BF16)
                lines[side, 1, rows, HALF:] = (imag_w[:, :HALF] - imag_w[:, HALF:]).astype(BF16)
    scale = [1.0 / (NFFT * sigma) for sigma in sigmas]
    for parity in range(2):
        for part in range(N2 // BLK):
            rows = pl.ds(part * BLK, BLK)
            network = 0.0
            for side in range(2):
                z = dot(lines[side, parity, rows, :], last[parity])
                network = network + (z[:, :HALF] * z[:, :HALF] + z[:, HALF:] * z[:, HALF:]) * scale[side]
            peaks[0, pl.ds(4 * parity + part, 1), :] = jnp.max(network, axis=0, keepdims=True)


VMEM_LIMIT = 56 * 1024 * 1024


def whole(shape):
    return pl.BlockSpec(shape, lambda step: (0,) * len(shape))


def scalar_spec():
    return pl.BlockSpec(memory_space=pltpu.SMEM)


def shards(tables, strain, inv_asd, templates, chirp_blocks, owner, slide):
    detector = lax.axis_index("det")
    group = lax.axis_index("grp")
    per_dev = templates.shape[0]
    n_det, n_grp, n_filt = lax.axis_size("det"), lax.axis_size("grp"), lax.axis_size("filt")
    mine = per_dev // n_det
    capacity = (per_dev + n_filt - 1) // n_filt
    swap = [(0, 1), (1, 0)]
    strain2d = strain.reshape(NBLK, BLK)
    weight_rows = inv_asd.reshape(NBLK // 2, BLK)
    strain_other = lax.ppermute(strain2d, "det", swap)
    weight_other = lax.ppermute(weight_rows, "det", swap)
    own_shift = jnp.where(detector == 1, slide[0], 0)
    other_shift = jnp.where(detector == 1, 0, slide[0])
    scalars_a = jnp.stack([own_shift, detector]).astype(jnp.int32)
    scalars_b = jnp.stack([other_shift, detector]).astype(jnp.int32)

    spec_shape, weight_shape = (2, N1, N1), (2, HALF, N1)
    common_scratch = [
        pltpu.VMEM((2 * NBLK, BLK), F32),
        pltpu.VMEM((N2, N1), BF16),
        pltpu.VMEM((2, N2, N1), BF16),
    ]
    bank, spec_own, weight_own = pl.pallas_call(
        bank_kernel,
        grid=(mine,),
        out_shape=(
            jax.ShapeDtypeStruct((mine,) + spec_shape, F32),
            jax.ShapeDtypeStruct(spec_shape, F32),
            jax.ShapeDtypeStruct(weight_shape, F32),
        ),
        in_specs=[
            scalar_spec(),
            scalar_spec(),
            whole(templates.shape),
            whole(strain2d.shape),
            whole(weight_rows.shape),
            whole(tables["spread"].shape),
            whole(tables["first"].shape),
            whole(tables["cos_twist"].shape),
            whole(tables["sin_twist"].shape),
            whole(tables["ahead"].shape),
        ],
        out_specs=(
            pl.BlockSpec((1,) + spec_shape, lambda step: (step, 0, 0, 0)),
            whole(spec_shape),
            whole(weight_shape),
        ),
        scratch_shapes=common_scratch
        + [
            pltpu.VMEM((ROWS * SLAB, N2), F32),
            pltpu.VMEM((N2, ROWS * SLAB), BF16),
        ],
        compiler_params=pltpu.CompilerParams(vmem_limit_bytes=VMEM_LIMIT),
        cost_estimate=pl.CostEstimate(flops=2_000_000_000, bytes_accessed=8_000_000, transcendentals=0),
        name="bank_spectra",
    )(
        scalars_a, chirp_blocks, templates, strain2d, weight_rows,
        tables["spread"], tables["first"], tables["cos_twist"], tables["sin_twist"], tables["ahead"],
    )

    maxima = pl.pallas_call(
        filter_kernel,
        grid=(mine,),
        out_shape=jax.ShapeDtypeStruct((mine, 8, HALF), F32),
        in_specs=[
            scalar_spec(),
            pl.BlockSpec((1,) + spec_shape, lambda step: (step, 0, 0, 0)),
            whole(spec_shape),
            whole(weight_shape),
            whole(strain2d.shape),
            whole(weight_rows.shape),
            whole(tables["first"].shape),
            whole(tables["cos_twist"].shape),
            whole(tables["sin_twist"].shape),
            whole(tables["ahead"].shape),
            whole(tables["back"].shape),
            whole(tables["last"].shape),
        ],
        out_specs=pl.BlockSpec((1, 8, HALF), lambda step: (step, 0, 0)),
        scratch_shapes=[pltpu.VMEM(spec_shape, F32), pltpu.VMEM(weight_shape, F32)]
        + common_scratch
        + [
            pltpu.VMEM((2, N1, N1), BF16),
            pltpu.VMEM((2, 2, N2, N1), BF16),
        ],
        compiler_params=pltpu.CompilerParams(vmem_limit_bytes=VMEM_LIMIT),
        cost_estimate=pl.CostEstimate(flops=4_000_000_000, bytes_accessed=8_000_000, transcendentals=0),
        name="matched_filter",
    )(
        scalars_b, bank, spec_own, weight_own, strain_other, weight_other,
        tables["first"], tables["cos_twist"], tables["sin_twist"], tables["ahead"], tables["back"], tables["last"],
    )

    half = NBLK // n_det
    rows = maxima.transpose(0, 2, 1).reshape(mine, NBLK)
    positions = jnp.arange(per_dev, dtype=jnp.int32)
    same_owner = owner[:, None] == owner[None, :]
    earlier = positions[None, :] < positions[:, None]
    rank = jnp.sum(jnp.logical_and(same_owner, earlier).astype(jnp.int32), axis=1)
    slot = lax.dynamic_slice_in_dim(owner * capacity + rank, detector * mine, mine)
    slots = n_filt * capacity
    placing = jnp.arange(slots, dtype=jnp.int32)[:, None] == slot[None, :]
    placed = jnp.max(jnp.where(placing[:, :, None], rows[None], -1.0), axis=1)
    placed = placed.reshape(n_filt, capacity, n_det, half).transpose(2, 0, 1, 3)
    placed = jnp.broadcast_to(placed[:, None], (n_det, n_grp, n_filt, capacity, half))
    top = jnp.max(rows, axis=0).reshape(n_det, 1, 1, 1, half)
    top = jnp.broadcast_to(top, (n_det, n_grp, n_filt, 1, half))
    send = jnp.concatenate([placed, top], axis=3).reshape(n_det * n_grp * n_filt, capacity + 1, half)
    got = lax.all_to_all(send, ("det", "grp", "filt"), split_axis=0, concat_axis=0, tiled=True)
    got = got.reshape(n_det, n_grp, n_filt, capacity + 1, half)
    loudest = jnp.max(got[:, :, :, capacity], axis=(0, 1, 2))
    own_group = lax.dynamic_slice_in_dim(got[:, :, :, :capacity], group, 1, axis=1)
    landed = jnp.max(own_group[:, 0], axis=0).reshape(slots, half)
    if slots == per_dev:
        return landed, loudest
    valid = landed[:, 0] >= 0.0
    order = jnp.cumsum(valid.astype(jnp.int32)) - 1
    picker = jnp.logical_and(valid[None, :], order[None, :] == positions[:, None])
    return jnp.max(jnp.where(picker[:, :, None], landed[None], 0.0), axis=1), loudest


def solution(mesh):
    tables = make_tables()
    return jax.shard_map(
        functools.partial(shards, tables),
        mesh=mesh,
        in_specs=(
            P("det", None),
            P("det", None),
            P(("grp", "filt"), None),
            P(("grp", "filt")),
            P(("grp", "filt")),
            P("grp"),
        ),
        out_specs=(P(("grp", "filt"), "det"), P("det")),
        check_vma=False,
    )
```

```python
import functools

import jax
import jax.numpy as jnp
import ml_dtypes
import numpy as np
from jax import lax
from jax.experimental import pallas as pl
from jax.experimental.pallas import tpu as pltpu
from jax.sharding import PartitionSpec as P

N1 = 256
N2 = 512
NFFT = 131072
BLK = 128
NBLK = 1024
TL = 4096
ROWS = TL // N2
SLAB = 16
HALF = 128
BF16 = jnp.bfloat16
F32 = jnp.float32


def wave(left, right, period):
    angle = 2.0 * np.pi * ((np.asarray(left)[:, None] * np.asarray(right)[None, :]) % period) / period
    return np.cos(angle).astype(np.float32), np.sin(angle).astype(np.float32)


def make_tables():
    ar = np.arange
    cos_first, sin_first = wave(ar(N1), ar(N1), N1)
    first = np.concatenate([cos_first, -sin_first], axis=1)
    spread = np.repeat(first[:ROWS], SLAB, axis=0)
    cos_twist, sin_twist = wave(ar(N2), ar(N1), NFFT)
    ahead, back, last = [], [], []
    for parity in range(2):
        bins = 2 * ar(HALF) + parity
        cos_m, sin_m = wave(bins, ar(N1), N2)
        ahead.append(np.block([[cos_m, sin_m], [-sin_m, cos_m]]))
        back.append(np.block([[cos_m.T, -sin_m.T], [sin_m.T, cos_m.T]]))
        cos_l, sin_l = wave(ar(HALF), bins, N1)
        last.append(np.block([[cos_l, sin_l], [-sin_l, cos_l]]))
    low = lambda value: np.asarray(value, dtype=ml_dtypes.bfloat16)
    return dict(
        first=low(first),
        spread=low(spread),
        cos_twist=cos_twist,
        sin_twist=sin_twist,
        ahead=low(np.stack(ahead)),
        back=low(np.stack(back)),
        last=low(np.stack(last)),
        spread_rows=low(np.tile(np.eye(8), (1, HALF // 8))),
    )


def dot(left, right):
    return jnp.dot(left, right, preferred_element_type=F32)


FWD_CHUNK = 256
INV_CHUNK = 256


def forward(signal, first, cos_t, sin_t, ahead, folded):
    for start in range(0, N1, FWD_CHUNK):
        parts = []
        for base in (start, start + N1):
            rows = pl.ds(base, FWD_CHUNK)
            both = dot(signal[rows, :], first)
            real_a, imag_a = both[:, :N1], both[:, N1:]
            cos_c, sin_c = cos_t[rows, :], sin_t[rows, :]
            parts.append((real_a * cos_c + imag_a * sin_c, imag_a * cos_c - real_a * sin_c))
        (real_l, imag_l), (real_u, imag_u) = parts
        folded[0, pl.ds(start, FWD_CHUNK), :] = (real_l + real_u).astype(BF16)
        folded[0, pl.ds(start + N1, FWD_CHUNK), :] = (imag_l + imag_u).astype(BF16)
        folded[1, pl.ds(start, FWD_CHUNK), :] = (real_l - real_u).astype(BF16)
        folded[1, pl.ds(start + N1, FWD_CHUNK), :] = (imag_l - imag_u).astype(BF16)
    return dot(ahead[0], folded[0]), dot(ahead[1], folded[1])


def data_spectrum(shift, strain, weight, first, cos_t, sin_t, ahead, twice, flipped, folded, spec, weight2d):
    twice[pl.ds(0, NBLK), :] = strain[...]
    twice[pl.ds(NBLK, NBLK), :] = strain[...]
    for part in range(N2 // BLK):
        block = twice[pl.ds(shift + part, N1, stride=N2 // BLK), :]
        flipped[pl.ds(part * BLK, BLK), :] = block.T.astype(BF16)
    halves = forward(flipped, first[...], cos_t, sin_t, ahead, folded)
    for parity in range(2):
        for part in range(2):
            weight2d[parity, :, pl.ds(part * HALF, HALF)] = weight[pl.ds(2 * parity + part, HALF, stride=4), :]
        kept = weight2d[parity]
        spec[parity, pl.ds(0, HALF), :] = halves[parity][:HALF] * kept
        spec[parity, pl.ds(HALF, HALF), :] = halves[parity][HALF:] * kept


def bank_kernel(slide, blocks, templates, strain, weight, spread, first, cos_t, sin_t, ahead,
                bank, spec, weight2d, twice, flipped, folded, slabs, bank_t):
    step = pl.program_id(0)
    mine = pl.num_programs(0)
    total = templates.shape[0]
    detector = lax.axis_index("det")

    @pl.when(step == 0)
    def _():
        slabs[...] = jnp.zeros_like(slabs)
        row = lax.broadcasted_iota(jnp.int32, (total, N2), 0)
        column = lax.broadcasted_iota(jnp.int32, (total, N2), 1)
        limit = jnp.zeros((total, N2), jnp.int32)
        for index in range(total):
            limit = jnp.where(row == index, BLK * blocks[index], limit)
        for part in range(ROWS):
            piece = templates[:, pl.ds(part * N2, N2)].astype(F32)
            slabs[pl.ds(part * SLAB, total), :] = jnp.where(column + part * N2 < limit, piece, 0.0)
        bank_t[...] = slabs[...].T.astype(BF16)
        data_spectrum(detector * slide[0], strain, weight, first, cos_t, sin_t, ahead, twice, flipped, folded, spec, weight2d)

    slot = lax.broadcasted_iota(jnp.int32, spread.shape, 0) % SLAB
    picked = jnp.where(slot == detector * mine + step, spread[...].astype(F32), 0.0).astype(BF16)
    even, odd = forward(bank_t, picked, cos_t, sin_t, ahead, folded)
    bank[0, 0] = even
    bank[0, 1] = odd


def pack_peaks(detector, owner, spread_rows, peaks, slots, send):
    mine, per_dev = peaks.shape[0], owner.shape[0]
    n_filt, capacity = slots.shape[:2]
    n_det = per_dev // mine
    slots[...] = jnp.full(slots.shape, -1.0, F32)
    lane = lax.broadcasted_iota(jnp.int32, (HALF, HALF), 1)
    row = lax.broadcasted_iota(jnp.int32, (HALF, HALF), 0)
    kept = lane // 8 == row % 16
    top = None
    for index in range(mine):
        turned = peaks[index].astype(BF16).astype(F32).T.astype(BF16)
        wide = dot(turned, spread_rows[...])
        ordered = jnp.sum(jnp.where(kept, wide, 0.0).reshape(8, 16, HALF), axis=1)
        top = ordered if top is None else jnp.maximum(top, ordered)
        here = detector * mine + index
        target = owner[here]
        rank = 0
        for other in range(per_dev):
            rank = rank + jnp.where(jnp.logical_and(owner[other] == target, other < here), 1, 0)
        slots[target, rank] = ordered
    rows = NBLK // BLK // n_det
    pad = send.shape[1] - rows * (capacity + 1)
    for half in range(n_det):
        span = slice(half * rows, (half + 1) * rows)
        for place in range(n_filt):
            parts = [slots[place, rank, span] for rank in range(capacity)] + [top[span]]
            if pad:
                parts.append(jnp.full((pad, HALF), -1.0, F32))
            chunk = jnp.concatenate(parts, axis=0).astype(BF16)
            for turn in range(send.shape[0] // (n_det * n_filt)):
                send[(half * (send.shape[0] // (n_det * n_filt)) + turn) * n_filt + place] = chunk


def filter_kernel(slide, owner, bank, spec_own, weight_own, strain, weight, first, cos_t, sin_t, ahead, back, last, spread_rows,
                  send, spec, weight2d, twice, flipped, folded, product, lines, peaks, slots):
    step = pl.program_id(0)
    mine = pl.num_programs(0)
    detector = lax.axis_index("det")

    @pl.when(step == 0)
    def _():
        shift = (1 - detector) * slide[0]
        data_spectrum(shift, strain, weight, first, cos_t, sin_t, ahead, twice, flipped, folded, spec, weight2d)

    sigmas = []
    for side, (spectrum, weights) in enumerate(((spec_own, weight_own), (spec, weight2d))):
        sigma = jnp.zeros((1, 1), F32)
        for parity in range(2):
            bank_r, bank_i = bank[0, parity, :HALF], bank[0, parity, HALF:]
            data_r, data_i = spectrum[parity, :HALF], spectrum[parity, HALF:]
            kept = weights[parity]
            power = kept * kept * (bank_r * bank_r + bank_i * bank_i)
            sigma = sigma + jnp.sum(jnp.sum(power, axis=0, keepdims=True), axis=1, keepdims=True)
            product[parity, pl.ds(0, HALF), :] = (bank_r * data_r + bank_i * data_i).astype(BF16)
            product[parity, pl.ds(HALF, HALF), :] = (bank_r * data_i - bank_i * data_r).astype(BF16)
        sigmas.append(sigma)
        for start in range(0, N1, INV_CHUNK):
            low, high = pl.ds(start, INV_CHUNK), pl.ds(start + N1, INV_CHUNK)
            real_e, imag_e = dot(back[0, low, :], product[0]), dot(back[0, high, :], product[0])
            real_o, imag_o = dot(back[1, low, :], product[1]), dot(back[1, high, :], product[1])
            for rows, real_d, imag_d in ((low, real_e + real_o, imag_e + imag_o), (high, real_e - real_o, imag_e - imag_o)):
                cos_c, sin_c = cos_t[rows, :], sin_t[rows, :]
                real_w = real_d * cos_c - imag_d * sin_c
                imag_w = real_d * sin_c + imag_d * cos_c
                lines[side, 0, rows, :HALF] = (real_w[:, :HALF] + real_w[:, HALF:]).astype(BF16)
                lines[side, 0, rows, HALF:] = (imag_w[:, :HALF] + imag_w[:, HALF:]).astype(BF16)
                lines[side, 1, rows, :HALF] = (real_w[:, :HALF] - real_w[:, HALF:]).astype(BF16)
                lines[side, 1, rows, HALF:] = (imag_w[:, :HALF] - imag_w[:, HALF:]).astype(BF16)
    scale = [1.0 / (NFFT * sigma) for sigma in sigmas]
    for parity in range(2):
        for part in range(N2 // BLK):
            rows = pl.ds(part * BLK, BLK)
            network = 0.0
            for side in range(2):
                z = dot(lines[side, parity, rows, :], last[parity])
                network = network + (z[:, :HALF] * z[:, :HALF] + z[:, HALF:] * z[:, HALF:]) * scale[side]
            peaks[step, pl.ds(4 * parity + part, 1), :] = jnp.max(network, axis=0, keepdims=True)

    @pl.when(step == mine - 1)
    def _():
        pack_peaks(detector, owner, spread_rows, peaks, slots, send)


VMEM_LIMIT = 56 * 1024 * 1024


def whole(shape):
    return pl.BlockSpec(shape, lambda step: (0,) * len(shape))


def scalar_spec():
    return pl.BlockSpec(memory_space=pltpu.SMEM)


def shards(tables, strain, inv_asd, templates, chirp_blocks, owner, slide):
    detector = lax.axis_index("det")
    group = lax.axis_index("grp")
    per_dev = templates.shape[0]
    n_det, n_grp, n_filt = lax.axis_size("det"), lax.axis_size("grp"), lax.axis_size("filt")
    mine = per_dev // n_det
    capacity = (per_dev + n_filt - 1) // n_filt
    swap = [(0, 1), (1, 0)]
    strain2d = strain.reshape(NBLK, BLK)
    weight_rows = inv_asd.reshape(NBLK // 2, BLK)
    strain_other = lax.ppermute(strain2d, "det", swap)
    weight_other = lax.ppermute(weight_rows, "det", swap)
    spec_shape, weight_shape = (2, N1, N1), (2, HALF, N1)
    common_scratch = [
        pltpu.VMEM((2 * NBLK, BLK), F32),
        pltpu.VMEM((N2, N1), BF16),
        pltpu.VMEM((2, N2, N1), BF16),
    ]
    bank, spec_own, weight_own = pl.pallas_call(
        bank_kernel,
        grid=(mine,),
        out_shape=(
            jax.ShapeDtypeStruct((mine,) + spec_shape, F32),
            jax.ShapeDtypeStruct(spec_shape, F32),
            jax.ShapeDtypeStruct(weight_shape, F32),
        ),
        in_specs=[
            scalar_spec(),
            scalar_spec(),
            whole(templates.shape),
            whole(strain2d.shape),
            whole(weight_rows.shape),
            whole(tables["spread"].shape),
            whole(tables["first"].shape),
            whole(tables["cos_twist"].shape),
            whole(tables["sin_twist"].shape),
            whole(tables["ahead"].shape),
        ],
        out_specs=(
            pl.BlockSpec((1,) + spec_shape, lambda step: (step, 0, 0, 0)),
            whole(spec_shape),
            whole(weight_shape),
        ),
        scratch_shapes=common_scratch
        + [
            pltpu.VMEM((ROWS * SLAB, N2), F32),
            pltpu.VMEM((N2, ROWS * SLAB), BF16),
        ],
        compiler_params=pltpu.CompilerParams(vmem_limit_bytes=VMEM_LIMIT),
        cost_estimate=pl.CostEstimate(flops=2_000_000_000, bytes_accessed=8_000_000, transcendentals=0),
        name="bank_spectra",
    )(
        slide, chirp_blocks, templates, strain2d, weight_rows,
        tables["spread"], tables["first"], tables["cos_twist"], tables["sin_twist"], tables["ahead"],
    )

    half = NBLK // n_det
    rows = half // BLK
    depth = -(-rows * (capacity + 1) // 16) * 16
    everyone = n_det * n_grp * n_filt
    send = pl.pallas_call(
        filter_kernel,
        grid=(mine,),
        out_shape=jax.ShapeDtypeStruct((everyone, depth, BLK), BF16),
        in_specs=[
            scalar_spec(),
            scalar_spec(),
            pl.BlockSpec((1,) + spec_shape, lambda step: (step, 0, 0, 0)),
            whole(spec_shape),
            whole(weight_shape),
            whole(strain2d.shape),
            whole(weight_rows.shape),
            whole(tables["first"].shape),
            whole(tables["cos_twist"].shape),
            whole(tables["sin_twist"].shape),
            whole(tables["ahead"].shape),
            whole(tables["back"].shape),
            whole(tables["last"].shape),
            whole(tables["spread_rows"].shape),
        ],
        out_specs=whole((everyone, depth, BLK)),
        scratch_shapes=[pltpu.VMEM(spec_shape, F32), pltpu.VMEM(weight_shape, F32)]
        + common_scratch
        + [
            pltpu.VMEM((2, N1, N1), BF16),
            pltpu.VMEM((2, 2, N2, N1), BF16),
            pltpu.VMEM((mine, 8, HALF), F32),
            pltpu.VMEM((n_filt, capacity, 8, HALF), F32),
        ],
        compiler_params=pltpu.CompilerParams(vmem_limit_bytes=VMEM_LIMIT),
        cost_estimate=pl.CostEstimate(flops=4_000_000_000, bytes_accessed=8_000_000, transcendentals=0),
        name="matched_filter",
    )(
        slide, owner, bank, spec_own, weight_own, strain_other, weight_other,
        tables["first"], tables["cos_twist"], tables["sin_twist"], tables["ahead"], tables["back"], tables["last"],
        tables["spread_rows"],
    )

    got = lax.all_to_all(send, ("det", "grp", "filt"), split_axis=0, concat_axis=0, tiled=True)
    got = got.reshape(n_det, n_grp, n_filt, depth, BLK)
    loudest = jnp.max(got[:, :, :, rows * capacity : rows * (capacity + 1)], axis=(0, 1, 2)).reshape(half).astype(F32)
    own_group = lax.dynamic_slice_in_dim(got[:, :, :, : rows * capacity], group, 1, axis=1)
    landed = jnp.max(own_group[:, 0], axis=0).reshape(n_filt * capacity, half).astype(F32)
    slots = n_filt * capacity
    if slots == per_dev:
        return landed, loudest
    positions = jnp.arange(per_dev, dtype=jnp.int32)
    valid = landed[:, 0] >= 0.0
    order = jnp.cumsum(valid.astype(jnp.int32)) - 1
    picker = jnp.logical_and(valid[None, :], order[None, :] == positions[:, None])
    return jnp.max(jnp.where(picker[:, :, None], landed[None], 0.0), axis=1), loudest


def solution(mesh):
    tables = make_tables()
    return jax.shard_map(
        functools.partial(shards, tables),
        mesh=mesh,
        in_specs=(
            P("det", None),
            P("det", None),
            P(("grp", "filt"), None),
            P(("grp", "filt")),
            P(("grp", "filt")),
            P("grp"),
        ),
        out_specs=(P(("grp", "filt"), "det"), P("det")),
        check_vma=False,
    )
```

```python
import functools

import jax
import jax.numpy as jnp
import ml_dtypes
import numpy as np
from jax import lax
from jax.experimental import pallas as pl
from jax.experimental.pallas import tpu as pltpu
from jax.sharding import PartitionSpec as P

N1 = 256
N2 = 512
NFFT = 131072
BLK = 128
NBLK = 1024
TL = 4096
ROWS = TL // N2
SLAB = 16
HALF = 128
CHUNK = 16
ORDER_BLOCKS = 3
BF16 = jnp.bfloat16
F32 = jnp.float32
VMEM_LIMIT = 16 * 1024 * 1024


def wave(left, right, period):
    angle = 2.0 * np.pi * ((np.asarray(left)[:, None] * np.asarray(right)[None, :]) % period) / period
    return np.cos(angle).astype(np.float32), np.sin(angle).astype(np.float32)


def make_tables():
    ar = np.arange
    cos_first, sin_first = wave(ar(N1), ar(N1), N1)
    first = np.concatenate([cos_first, -sin_first], axis=1)
    spread = np.repeat(first[:ROWS], SLAB, axis=0)
    cos_twist, sin_twist = wave(ar(N2), ar(N1), NFFT)
    ahead, back, last = [], [], []
    for parity in range(2):
        bins = 2 * ar(HALF) + parity
        cos_m, sin_m = wave(bins, ar(N1), N2)
        ahead.append(np.block([[cos_m, sin_m], [-sin_m, cos_m]]))
        pairs = np.block([[cos_m.T, -sin_m.T], [sin_m.T, cos_m.T]]).reshape(2, N1 // CHUNK, CHUNK, N1)
        back.append(pairs.transpose(1, 0, 2, 3).reshape(2 * N1, N1))
        cos_l, sin_l = wave(ar(HALF), bins, N1)
        last.append(np.block([[cos_l, sin_l], [-sin_l, cos_l]]))
    order = np.kron(np.eye(HALF // 8), np.tile(np.eye(8), (1, HALF // 8)))
    order = [order[:, start : start + N1] for start in range(0, order.shape[1], N1)]
    low = lambda parts: np.concatenate(parts).astype(ml_dtypes.bfloat16)
    return low([cos_twist, sin_twist]), low([spread] + ahead + [first]), low(back + last + order[:ORDER_BLOCKS])


def wide_parts(wide):
    return wide.at[pl.ds(0, HALF)], (wide.at[pl.ds(HALF, N1)], wide.at[pl.ds(HALF + N1, N1)]), wide.at[pl.ds(HALF + 2 * N1, N1)]


def tall_parts(tall):
    back = (tall.at[pl.ds(0, N2)], tall.at[pl.ds(N2, N2)])
    last = (tall.at[pl.ds(2 * N2, N1)], tall.at[pl.ds(2 * N2 + N1, N1)])
    return back, last, [tall.at[pl.ds(3 * N2 + index * HALF, HALF)] for index in range(ORDER_BLOCKS)]


def dot(left, right):
    return jnp.dot(left, right, preferred_element_type=F32)


def woven(index):
    halves = N1 // CHUNK
    return (2 * (index % halves) + index // halves) * CHUNK


def forward(signal, first, twist, ahead, folded, before_twist=None):
    both = dot(signal[...], first)
    if before_twist is not None:
        before_twist()
    for chunk in range(N1 // CHUNK):
        parts = []
        for half in range(2):
            base = (2 * chunk + half) * CHUNK
            real_a, imag_a = both[base : base + CHUNK, :N1], both[base : base + CHUNK, N1:]
            rows = pl.ds(half * N1 + chunk * CHUNK, CHUNK)
            cos_c, sin_c = twist[rows, :], twist[pl.ds(N2 + half * N1 + chunk * CHUNK, CHUNK), :]
            parts.append((real_a * cos_c + imag_a * sin_c, imag_a * cos_c - real_a * sin_c))
        (real_l, imag_l), (real_u, imag_u) = parts
        real, imag = pl.ds(chunk * CHUNK, CHUNK), pl.ds(N1 + chunk * CHUNK, CHUNK)
        folded[0, real, :] = (real_l + real_u).astype(BF16)
        folded[0, imag, :] = (imag_l + imag_u).astype(BF16)
        folded[1, real, :] = (real_l - real_u).astype(BF16)
        folded[1, imag, :] = (imag_l - imag_u).astype(BF16)
    return dot(ahead[0][...], folded[0]), dot(ahead[1][...], folded[1])


def data_spectrum(shift, strain, weight, first, twist, ahead, twice, flipped, folded, data, before_twist):
    twice[pl.ds(0, NBLK), :] = strain[...]
    twice[pl.ds(NBLK, NBLK), :] = strain[...]
    for part in range(N2 // BLK):
        block = twice[pl.ds(shift + part, N1, stride=N2 // BLK), :].T.astype(BF16)
        for chunk in range(BLK // CHUNK):
            flipped[pl.ds(woven(part * (BLK // CHUNK) + chunk), CHUNK), :] = block[chunk * CHUNK : (chunk + 1) * CHUNK]
    halves = forward(flipped, first[...], twist, ahead, folded, before_twist)
    for parity in range(2):
        for part in range(2):
            lanes = slice(part * HALF, (part + 1) * HALF)
            kept = weight[pl.ds(2 * parity + part, HALF, stride=4), :]
            data[2, pl.ds(parity * HALF, HALF), lanes] = (kept * kept).astype(BF16)
            data[parity, :HALF, lanes] = (halves[parity][:HALF, lanes] * kept).astype(BF16)
            data[parity, HALF:, lanes] = (halves[parity][HALF:, lanes] * kept).astype(BF16)


def fetches(pairs, sems):
    return [pltpu.make_async_copy(source, target, sems.at[index]) for index, (source, target) in enumerate(pairs)]


def start_all(copies):
    for copy in copies:
        copy.start()


def wait_all(copies):
    for copy in copies:
        copy.wait()


def data_kernel(slide, blocks_hbm, templates_hbm, strain_hbm, weight_hbm, twist_low_hbm, wide_hbm,
                data, bank_t, twist, twist_low, wide,
                blocks, templates, strain, weight, twice, flipped, folded, slabs, sems):
    total = templates.shape[0]
    detector = lax.axis_index("det")
    _, ahead, first = wide_parts(wide)
    copies = fetches(
        (
            (blocks_hbm, blocks),
            (templates_hbm, templates),
            (strain_hbm, strain),
            (wide_hbm, wide),
            (twist_low_hbm, twist_low),
            (weight_hbm, weight),
        ),
        sems,
    )
    start_all(copies)

    def before_twist():
        copies[4].wait()
        twist[...] = twist_low[...].astype(F32)
        copies[5].wait()

    slabs[...] = jnp.zeros_like(slabs)
    row = lax.broadcasted_iota(jnp.int32, (total, N2), 0)
    column = lax.broadcasted_iota(jnp.int32, (total, N2), 1)
    wait_all(copies[:2])
    limit = jnp.zeros((total, N2), jnp.int32)
    for index in range(total):
        limit = jnp.where(row == index, BLK * blocks[index], limit)
    for part in range(ROWS):
        piece = templates[:, pl.ds(part * N2, N2)].astype(F32)
        slabs[pl.ds(part * SLAB, total), :] = jnp.where(column + part * N2 < limit, piece, 0.0)
    turned = slabs[...].T.astype(BF16)
    for chunk in range(N2 // CHUNK):
        bank_t[pl.ds(woven(chunk), CHUNK), :] = turned[chunk * CHUNK : (chunk + 1) * CHUNK]
    wait_all(copies[2:4])
    shift = detector * slide[0]
    data_spectrum(shift, strain, weight, first, twist, ahead, twice, flipped, folded, data, before_twist)


def bank_kernel(bank_t, twist, wide, bank, folded):
    mine = bank.shape[0]
    detector = lax.axis_index("det")
    spread, ahead, _ = wide_parts(wide)
    place = lax.broadcasted_iota(jnp.int32, spread.shape, 0) % SLAB
    for index in range(mine):
        picked = jnp.where(place == detector * mine + index, spread[...].astype(F32), 0.0).astype(BF16)
        halves = forward(bank_t, picked, twist, ahead, folded.at[index % 2])
        for parity in range(2):
            bank[index, parity] = halves[parity].astype(BF16)


def multiply(bank, data, product):
    power = jnp.zeros((8, N1), F32)
    for parity in range(2):
        pending = None
        for start in range(0, HALF, CHUNK):
            real, imag = pl.ds(start, CHUNK), pl.ds(HALF + start, CHUNK)
            bank_r, bank_i = bank[parity, real, :], bank[parity, imag, :]
            data_r, data_i = data[parity, real, :], data[parity, imag, :]
            each = data[2, pl.ds(parity * HALF + start, CHUNK), :] * (bank_r * bank_r + bank_i * bank_i)
            pending = each if pending is None else pending + each
            if start // CHUNK % 2 == 1:
                power = power + jnp.sum(pending.astype(F32).reshape(CHUNK // 8, 8, N1), axis=0)
                pending = None
            product[parity, real, :] = bank_r * data_r + bank_i * data_i
            product[parity, imag, :] = bank_r * data_i - bank_i * data_r
    return jnp.sum(jnp.sum(power, axis=0, keepdims=True), axis=1, keepdims=True)


def inverse_long(product, back, twist, lines, side):
    even, odd = dot(back[0][...], product[0]), dot(back[1][...], product[1])
    for chunk in range(N1 // CHUNK):
        base = 2 * chunk * CHUNK
        real_e, imag_e = even[base : base + CHUNK], even[base + CHUNK : base + 2 * CHUNK]
        real_o, imag_o = odd[base : base + CHUNK], odd[base + CHUNK : base + 2 * CHUNK]
        for place, real_d, imag_d in (
            (chunk, real_e + real_o, imag_e + imag_o),
            (chunk + N1 // CHUNK, real_e - real_o, imag_e - imag_o),
        ):
            cos_c, sin_c = twist[pl.ds(place * CHUNK, CHUNK), :], twist[pl.ds(N2 + place * CHUNK, CHUNK), :]
            real_d, imag_d = real_d.astype(BF16), imag_d.astype(BF16)
            real_w = real_d * cos_c - imag_d * sin_c
            imag_w = real_d * sin_c + imag_d * cos_c
            rows = pl.ds((2 * place + side) * CHUNK, CHUNK)
            lines[0, rows, :HALF] = real_w[:, :HALF] + real_w[:, HALF:]
            lines[0, rows, HALF:] = imag_w[:, :HALF] + imag_w[:, HALF:]
            lines[1, rows, :HALF] = real_w[:, :HALF] - real_w[:, HALF:]
            lines[1, rows, HALF:] = imag_w[:, :HALF] - imag_w[:, HALF:]


def inverse_short(lines, last, ratio, scale, peaks, base_row, parities=(0, 1)):
    for parity in parities:
        z = dot(lines[parity], last[parity][...])
        for part in range(N2 // BLK):
            best = None
            for chunk in range(BLK // CHUNK):
                base = 2 * (part * BLK + chunk * CHUNK)
                own, other = z[base : base + CHUNK], z[base + CHUNK : base + 2 * CHUNK]
                network = own[:, :HALF] * own[:, :HALF] + own[:, HALF:] * own[:, HALF:]
                network = network + (other[:, :HALF] * other[:, :HALF] + other[:, HALF:] * other[:, HALF:]) * ratio
                most = jnp.max(network.reshape(CHUNK // 8, 8, HALF), axis=0)
                best = most if best is None else jnp.maximum(best, most)
            peaks[pl.ds(base_row + 4 * parity + part, 1), :] = jnp.max(best, axis=0, keepdims=True) * scale


def in_block_order(peaks, order, mine):
    lane = lax.broadcasted_iota(jnp.int32, (HALF, HALF), 1)
    row = lax.broadcasted_iota(jnp.int32, (HALF, HALF), 0)
    turned = peaks.T.astype(BF16)
    result = []
    for index in range(mine):
        if index % 2 == 0:
            wide = dot(turned, order[index // 2][...])
        kept = jnp.where(lane // 8 == row % 16, wide[:, index % 2 * HALF : (index % 2 + 1) * HALF], 0.0)
        result.append(jnp.sum(kept.reshape(8, 16, HALF), axis=1))
    return result


def filter_kernel(owner_hbm, bank, data_own, twist_low, tall, data_other,
                  send,
                  owner, product, lines, peaks, slots, sem):
    mine, per_dev = bank.shape[0], owner.shape[0]
    n_filt, capacity = slots.shape[:2]
    n_det = per_dev // mine
    detector = lax.axis_index("det")
    back, last, order = tall_parts(tall)
    owners = pltpu.make_async_copy(owner_hbm, owner, sem)
    owners.start()
    slots[...] = jnp.full(slots.shape, -1.0, F32)
    peaks[...] = jnp.zeros_like(peaks)
    sigmas, ratios = [None] * mine, [None] * mine

    def own_q(index):
        sigmas[index] = multiply(bank.at[index], data_own, product.at[index % 2, 0])

    def own_d(index):
        inverse_long(product.at[index % 2, 0], back, twist_low, lines.at[index % 2], 0)

    def other_q(index):
        sigma_other = multiply(bank.at[index], data_other, product.at[index % 2, 1])
        ratios[index] = sigmas[index] / sigma_other

    def other_d(index):
        inverse_long(product.at[index % 2, 1], back, twist_low, lines.at[index % 2], 1)

    def both_sides(index, parities=(0, 1)):
        scale = 1.0 / (NFFT * sigmas[index])
        inverse_short(lines.at[index % 2], last, ratios[index], scale, peaks, 8 * index, parities)

    def begin(index):
        own_q(index)
        own_d(index)
        other_q(index)
        other_d(index)

    begin(0)
    for index in range(mine):
        if index + 1 < mine:
            begin(index + 1)
        both_sides(index)
    owners.wait()
    top = None
    for index, ordered in enumerate(in_block_order(peaks[...], order, mine)):
        top = ordered if top is None else jnp.maximum(top, ordered)
        here = detector * mine + index
        target = owner[here]
        rank = 0
        for other in range(per_dev):
            rank = rank + jnp.where(jnp.logical_and(owner[other] == target, other < here), 1, 0)
        slots[target, rank] = ordered
    rows = NBLK // BLK // n_det
    pad = send.shape[1] - rows * (capacity + 1)
    n_grp = send.shape[0] // (n_det * n_filt)
    for half in range(n_det):
        span = slice(half * rows, (half + 1) * rows)
        for place in range(n_filt):
            parts = [slots[place, rank, span] for rank in range(capacity)] + [top[span]]
            if pad:
                parts.append(jnp.full((pad, HALF), -1.0, F32))
            chunk = jnp.concatenate(parts, axis=0).astype(BF16)
            for group in range(n_grp):
                send[(half * n_grp + group) * n_filt + place] = chunk


def land_kernel(got, peaks_hbm, loudest_hbm, peaks, loudest, sems):
    n_det, n_grp, n_filt = lax.axis_size("det"), lax.axis_size("grp"), lax.axis_size("filt")
    group = lax.axis_index("grp")
    capacity = peaks.shape[0] // n_filt
    rows = peaks.shape[1] // BLK
    for place in range(n_filt):
        chunk = got[group * n_filt + place].astype(F32)
        for det in range(1, n_det):
            chunk = jnp.maximum(chunk, got[(det * n_grp + group) * n_filt + place].astype(F32))
        for rank in range(capacity):
            for part in range(rows):
                line = rank * rows + part
                peaks[pl.ds(place * capacity + rank, 1), pl.ds(part * BLK, BLK)] = chunk[line : line + 1]
    first = pltpu.make_async_copy(peaks, peaks_hbm, sems.at[0])
    first.start()
    top = got[0].astype(F32)
    for source in range(1, got.shape[0]):
        top = jnp.maximum(top, got[source].astype(F32))
    for part in range(rows):
        line = capacity * rows + part
        loudest[:, pl.ds(part * BLK, BLK)] = top[line : line + 1]
    second = pltpu.make_async_copy(loudest, loudest_hbm, sems.at[1])
    second.start()
    first.wait()
    second.wait()


def shards(tables, strain, inv_asd, templates, chirp_blocks, owner, slide):
    per_dev = templates.shape[0]
    n_det, n_grp, n_filt = lax.axis_size("det"), lax.axis_size("grp"), lax.axis_size("filt")
    mine = per_dev // n_det
    capacity = (per_dev + n_filt - 1) // n_filt
    swap = [(0, 1), (1, 0)]
    strain2d = strain.reshape(NBLK, BLK)
    weight_rows = inv_asd.reshape(NBLK // 2, BLK)
    vmem = pl.BlockSpec(memory_space=pltpu.VMEM)
    hbm = pl.BlockSpec(memory_space=pltpu.HBM)
    smem = pl.BlockSpec(memory_space=pltpu.SMEM)
    far = lambda value: pltpu.with_memory_space_constraint(value, pltpu.HBM)
    like = lambda value: pltpu.VMEM(value.shape, value.dtype)
    shape = jax.ShapeDtypeStruct
    params = pltpu.CompilerParams(vmem_limit_bytes=VMEM_LIMIT)
    twist_low, wide, tall = tables
    arrays = [templates, strain2d, weight_rows]
    data_own, bank_t, twist, twist_low, wide = pl.pallas_call(
        data_kernel,
        out_shape=[
            shape((3, N1, N1), BF16),
            shape((N2, ROWS * SLAB), BF16),
            shape(twist_low.shape, F32),
            shape(twist_low.shape, BF16),
            shape(wide.shape, BF16),
        ],
        in_specs=[smem] + [hbm] * 6,
        out_specs=[vmem] * 5,
        scratch_shapes=[pltpu.SMEM(chirp_blocks.shape, jnp.int32)]
        + [like(value) for value in arrays]
        + [
            pltpu.VMEM((2 * NBLK, BLK), F32),
            pltpu.VMEM((N2, N1), BF16),
            pltpu.VMEM((2, N2, N1), BF16),
            pltpu.VMEM((ROWS * SLAB, N2), F32),
            pltpu.SemaphoreType.DMA((6,)),
        ],
        compiler_params=params,
        cost_estimate=pl.CostEstimate(flops=500_000_000, bytes_accessed=4_000_000, transcendentals=0),
        name="data_spectrum",
    )(slide, *[far(value) for value in (chirp_blocks, *arrays, twist_low, wide)])
    data_other = lax.ppermute(data_own, "det", swap)
    bank = pl.pallas_call(
        bank_kernel,
        out_shape=shape((mine, 2, N1, N1), BF16),
        in_specs=[vmem] * 3,
        out_specs=vmem,
        scratch_shapes=[pltpu.VMEM((2, 2, N2, N1), BF16)],
        compiler_params=params,
        cost_estimate=pl.CostEstimate(flops=2_000_000_000, bytes_accessed=4_000_000, transcendentals=0),
        name="bank_spectra",
    )(bank_t, twist, wide)

    half = NBLK // n_det
    rows = half // BLK
    depth = -(-rows * (capacity + 1) // 16) * 16
    everyone = n_det * n_grp * n_filt
    send = pl.pallas_call(
        filter_kernel,
        out_shape=shape((everyone, depth, BLK), BF16),
        in_specs=[hbm] + [vmem] * 5,
        out_specs=vmem,
        scratch_shapes=[
            pltpu.SMEM(owner.shape, jnp.int32),
            pltpu.VMEM((2, 2, 2, N1, N1), BF16),
            pltpu.VMEM((2, 2, 2 * N2, N1), BF16),
            pltpu.VMEM((HALF, HALF), F32),
            pltpu.VMEM((n_filt, capacity, 8, HALF), F32),
            pltpu.SemaphoreType.DMA,
        ],
        compiler_params=params,
        cost_estimate=pl.CostEstimate(flops=4_000_000_000, bytes_accessed=8_000_000, transcendentals=0),
        name="matched_filter",
    )(far(owner), bank, data_own, twist_low, tall, data_other)

    got = lax.all_to_all(send, ("det", "grp", "filt"), split_axis=0, concat_axis=0, tiled=True)
    slots = n_filt * capacity
    landed, loudest = pl.pallas_call(
        land_kernel,
        out_shape=[jax.ShapeDtypeStruct((slots, half), F32), jax.ShapeDtypeStruct((1, half), F32)],
        in_specs=[vmem],
        out_specs=[hbm, hbm],
        scratch_shapes=[pltpu.VMEM((slots, half), F32), pltpu.VMEM((1, half), F32), pltpu.SemaphoreType.DMA((2,))],
        compiler_params=pltpu.CompilerParams(vmem_limit_bytes=VMEM_LIMIT),
        name="land_peaks",
    )(got)
    loudest = loudest.reshape(half)
    if slots == per_dev:
        return landed, loudest
    positions = jnp.arange(per_dev, dtype=jnp.int32)
    valid = landed[:, 0] >= 0.0
    order = jnp.cumsum(valid.astype(jnp.int32)) - 1
    picker = jnp.logical_and(valid[None, :], order[None, :] == positions[:, None])
    return jnp.max(jnp.where(picker[:, :, None], landed[None], 0.0), axis=1), loudest


def solution(mesh):
    tables = make_tables()
    return jax.shard_map(
        functools.partial(shards, tables),
        mesh=mesh,
        in_specs=(
            P("det", None),
            P("det", None),
            P(("grp", "filt"), None),
            P(("grp", "filt")),
            P(("grp", "filt")),
            P("grp"),
        ),
        out_specs=(P(("grp", "filt"), "det"), P("det")),
        check_vma=False,
    )
```

```python
import functools

import jax
import jax.numpy as jnp
import ml_dtypes
import numpy as np
from jax import lax
from jax.experimental import pallas as pl
from jax.experimental.pallas import tpu as pltpu
from jax.sharding import PartitionSpec as P

N1 = 256
N2 = 512
NFFT = 131072
BLK = 128
NBLK = 1024
TL = 4096
ROWS = TL // N2
SLAB = 16
HALF = 128
CHUNK = 16
ORDER_BLOCKS = 3
BF16 = jnp.bfloat16
F32 = jnp.float32
VMEM_LIMIT = 16 * 1024 * 1024


def wave(left, right, period):
    angle = 2.0 * np.pi * ((np.asarray(left)[:, None] * np.asarray(right)[None, :]) % period) / period
    return np.cos(angle).astype(np.float32), np.sin(angle).astype(np.float32)


def make_tables():
    ar = np.arange
    cos_first, sin_first = wave(ar(N1), ar(N1), N1)
    first = np.concatenate([cos_first, -sin_first], axis=1)
    spread = np.repeat(first[:ROWS], SLAB, axis=0)
    cos_twist, sin_twist = wave(ar(N2), ar(N1), NFFT)
    ahead, back, last = [], [], []
    for parity in range(2):
        bins = 2 * ar(HALF) + parity
        cos_m, sin_m = wave(bins, ar(N1), N2)
        ahead.append(np.block([[cos_m, sin_m], [-sin_m, cos_m]]))
        pairs = np.block([[cos_m.T, -sin_m.T], [sin_m.T, cos_m.T]]).reshape(2, N1 // CHUNK, CHUNK, N1)
        back.append(pairs.transpose(1, 0, 2, 3).reshape(2 * N1, N1))
        cos_l, sin_l = wave(ar(HALF), bins, N1)
        last.append(np.block([[cos_l, sin_l], [-sin_l, cos_l]]))
    order = np.kron(np.eye(HALF // 8), np.tile(np.eye(8), (1, HALF // 8)))
    order = [order[:, start : start + N1] for start in range(0, order.shape[1], N1)]
    low = lambda parts: np.concatenate(parts).astype(ml_dtypes.bfloat16)
    return low([cos_twist, sin_twist]), low([spread] + ahead + [first]), low(back + last + order[:ORDER_BLOCKS])


def wide_parts(wide):
    return wide.at[pl.ds(0, HALF)], (wide.at[pl.ds(HALF, N1)], wide.at[pl.ds(HALF + N1, N1)]), wide.at[pl.ds(HALF + 2 * N1, N1)]


def tall_parts(tall):
    back = (tall.at[pl.ds(0, N2)], tall.at[pl.ds(N2, N2)])
    last = (tall.at[pl.ds(2 * N2, N1)], tall.at[pl.ds(2 * N2 + N1, N1)])
    return back, last, [tall.at[pl.ds(3 * N2 + index * HALF, HALF)] for index in range(ORDER_BLOCKS)]


def dot(left, right):
    return jnp.dot(left, right, preferred_element_type=F32)


def woven(index):
    halves = N1 // CHUNK
    return (2 * (index % halves) + index // halves) * CHUNK


def forward_first(signal, first, twist, folded, before_twist=None):
    both = dot(signal[...], first)
    if before_twist is not None:
        before_twist()
    for chunk in range(N1 // CHUNK):
        parts = []
        for half in range(2):
            base = (2 * chunk + half) * CHUNK
            real_a, imag_a = both[base : base + CHUNK, :N1], both[base : base + CHUNK, N1:]
            rows = pl.ds(half * N1 + chunk * CHUNK, CHUNK)
            cos_c, sin_c = twist[rows, :], twist[pl.ds(N2 + half * N1 + chunk * CHUNK, CHUNK), :]
            parts.append((real_a * cos_c + imag_a * sin_c, imag_a * cos_c - real_a * sin_c))
        (real_l, imag_l), (real_u, imag_u) = parts
        real, imag = pl.ds(chunk * CHUNK, CHUNK), pl.ds(N1 + chunk * CHUNK, CHUNK)
        folded[0, real, :] = (real_l + real_u).astype(BF16)
        folded[0, imag, :] = (imag_l + imag_u).astype(BF16)
        folded[1, real, :] = (real_l - real_u).astype(BF16)
        folded[1, imag, :] = (imag_l - imag_u).astype(BF16)


def forward_last(ahead, folded):
    return dot(ahead[0][...], folded[0]), dot(ahead[1][...], folded[1])


def data_spectrum(shift, weight, first, twist, ahead, twice, flipped, folded, data, before_twist):
    twice[pl.ds(NBLK, NBLK), :] = twice[pl.ds(0, NBLK), :]
    for part in range(N2 // BLK):
        block = twice[pl.ds(shift + part, N1, stride=N2 // BLK), :].astype(BF16).T
        for chunk in range(BLK // CHUNK):
            flipped[pl.ds(woven(part * (BLK // CHUNK) + chunk), CHUNK), :] = block[chunk * CHUNK : (chunk + 1) * CHUNK]
    forward_first(flipped, first[...], twist, folded, before_twist)
    halves = forward_last(ahead, folded)
    for parity in range(2):
        for part in range(2):
            lanes = slice(part * HALF, (part + 1) * HALF)
            kept = weight[pl.ds(2 * parity + part, HALF, stride=4), :]
            data[2, pl.ds(parity * HALF, HALF), lanes] = (kept * kept).astype(BF16)
            data[parity, :HALF, lanes] = (halves[parity][:HALF, lanes] * kept).astype(BF16)
            data[parity, HALF:, lanes] = (halves[parity][HALF:, lanes] * kept).astype(BF16)


def fetches(pairs, sems):
    return [pltpu.make_async_copy(source, target, sems.at[index]) for index, (source, target) in enumerate(pairs)]


def start_all(copies):
    for copy in copies:
        copy.start()


def wait_all(copies):
    for copy in copies:
        copy.wait()


def data_kernel(slide, blocks_hbm, templates_hbm, strain_hbm, weight_hbm, twist_low_hbm, wide_hbm,
                data, bank_t, twist, twist_low, wide,
                blocks, templates, weight, twice, flipped, folded, slabs, sems):
    total = templates.shape[0]
    detector = lax.axis_index("det")
    _, ahead, first = wide_parts(wide)
    copies = fetches(
        (
            (blocks_hbm, blocks),
            (templates_hbm, templates),
            (strain_hbm, twice.at[pl.ds(0, NBLK)]),
            (wide_hbm.at[pl.ds(HALF + 2 * N1, N1)], first),
            (wide_hbm.at[pl.ds(0, HALF + 2 * N1)], wide.at[pl.ds(0, HALF + 2 * N1)]),
            (twist_low_hbm, twist_low),
            (weight_hbm, weight),
        ),
        sems,
    )
    start_all(copies)

    def before_twist():
        copies[5].wait()
        twist[...] = twist_low[...].astype(F32)
        copies[4].wait()
        copies[6].wait()

    slabs[...] = jnp.zeros_like(slabs)
    row = lax.broadcasted_iota(jnp.int32, (total, N2), 0)
    column = lax.broadcasted_iota(jnp.int32, (total, N2), 1)
    wait_all(copies[:2])
    limit = jnp.zeros((total, N2), jnp.int32)
    for index in range(total):
        limit = jnp.where(row == index, BLK * blocks[index], limit)
    for part in range(ROWS):
        piece = templates[:, pl.ds(part * N2, N2)].astype(F32)
        slabs[pl.ds(part * SLAB, total), :] = jnp.where(column + part * N2 < limit, piece, 0.0)
    turned = slabs[...].astype(BF16).T
    for chunk in range(N2 // CHUNK):
        bank_t[pl.ds(woven(chunk), CHUNK), :] = turned[chunk * CHUNK : (chunk + 1) * CHUNK]
    wait_all(copies[2:4])
    shift = detector * slide[0]
    data_spectrum(shift, weight, first, twist, ahead, twice, flipped, folded, data, before_twist)


def bank_kernel(bank_t, twist, wide, bank, folded):
    mine = bank.shape[0]
    detector = lax.axis_index("det")
    spread, ahead, _ = wide_parts(wide)
    place = lax.broadcasted_iota(jnp.int32, spread.shape, 0) % SLAB

    def begin(index):
        picked = jnp.where(place == detector * mine + index, spread[...].astype(F32), 0.0).astype(BF16)
        forward_first(bank_t, picked, twist, folded.at[index % 2])

    begin(0)
    for index in range(mine):
        if index + 1 < mine:
            begin(index + 1)
        halves = forward_last(ahead, folded.at[index % 2])
        for parity in range(2):
            bank[index, parity] = halves[parity].astype(BF16)


def multiply(bank, data, product):
    power = jnp.zeros((8, N1), F32)
    for parity in range(2):
        pending = None
        for start in range(0, HALF, CHUNK):
            real, imag = pl.ds(start, CHUNK), pl.ds(HALF + start, CHUNK)
            bank_r, bank_i = bank[parity, real, :], bank[parity, imag, :]
            data_r, data_i = data[parity, real, :], data[parity, imag, :]
            each = data[2, pl.ds(parity * HALF + start, CHUNK), :] * (bank_r * bank_r + bank_i * bank_i)
            pending = each if pending is None else pending + each
            if start // CHUNK % 2 == 1:
                power = power + jnp.sum(pending.astype(F32).reshape(CHUNK // 8, 8, N1), axis=0)
                pending = None
            product[parity, real, :] = bank_r * data_r + bank_i * data_i
            product[parity, imag, :] = bank_r * data_i - bank_i * data_r
    return jnp.sum(jnp.sum(power, axis=0, keepdims=True), axis=1, keepdims=True)


def inverse_long(product, back, twist, lines, side):
    even, odd = dot(back[0][...], product[0]), dot(back[1][...], product[1])
    for chunk in range(N1 // CHUNK):
        base = 2 * chunk * CHUNK
        real_e, imag_e = even[base : base + CHUNK], even[base + CHUNK : base + 2 * CHUNK]
        real_o, imag_o = odd[base : base + CHUNK], odd[base + CHUNK : base + 2 * CHUNK]
        for place, real_d, imag_d in (
            (chunk, real_e + real_o, imag_e + imag_o),
            (chunk + N1 // CHUNK, real_e - real_o, imag_e - imag_o),
        ):
            cos_c, sin_c = twist[pl.ds(place * CHUNK, CHUNK), :], twist[pl.ds(N2 + place * CHUNK, CHUNK), :]
            real_d, imag_d = real_d.astype(BF16), imag_d.astype(BF16)
            real_w = real_d * cos_c - imag_d * sin_c
            imag_w = real_d * sin_c + imag_d * cos_c
            rows = pl.ds((2 * place + side) * CHUNK, CHUNK)
            lines[0, rows, :HALF] = real_w[:, :HALF] + real_w[:, HALF:]
            lines[0, rows, HALF:] = imag_w[:, :HALF] + imag_w[:, HALF:]
            lines[1, rows, :HALF] = real_w[:, :HALF] - real_w[:, HALF:]
            lines[1, rows, HALF:] = imag_w[:, :HALF] - imag_w[:, HALF:]


def inverse_short(lines, last, ratio, scale, peaks, base_row, parities=(0, 1)):
    for parity in parities:
        z = dot(lines[parity], last[parity][...])
        for part in range(N2 // BLK):
            best = None
            for chunk in range(BLK // CHUNK):
                base = 2 * (part * BLK + chunk * CHUNK)
                own, other = z[base : base + CHUNK], z[base + CHUNK : base + 2 * CHUNK]
                network = own[:, :HALF] * own[:, :HALF] + own[:, HALF:] * own[:, HALF:]
                network = network + (other[:, :HALF] * other[:, :HALF] + other[:, HALF:] * other[:, HALF:]) * ratio
                most = jnp.max(network.reshape(CHUNK // 8, 8, HALF), axis=0)
                best = most if best is None else jnp.maximum(best, most)
            peaks[pl.ds(base_row + 4 * parity + part, 1), :] = jnp.max(best, axis=0, keepdims=True) * scale


def in_block_order(peaks, order, mine):
    lane = lax.broadcasted_iota(jnp.int32, (HALF, HALF), 1)
    row = lax.broadcasted_iota(jnp.int32, (HALF, HALF), 0)
    turned = peaks.T.astype(BF16)
    result = []
    for index in range(mine):
        if index % 2 == 0:
            wide = dot(turned, order[index // 2][...])
        kept = jnp.where(lane // 8 == row % 16, wide[:, index % 2 * HALF : (index % 2 + 1) * HALF], 0.0)
        result.append(jnp.sum(kept.reshape(8, 16, HALF), axis=1))
    return result


def filter_kernel(owner_hbm, bank, data_own, twist_low, tall, data_other,
                  send,
                  owner, product, lines, peaks, slots, sem):
    mine, per_dev = bank.shape[0], owner.shape[0]
    n_filt, capacity = slots.shape[:2]
    n_det = per_dev // mine
    detector = lax.axis_index("det")
    back, last, order = tall_parts(tall)
    owners = pltpu.make_async_copy(owner_hbm, owner, sem)
    owners.start()
    slots[...] = jnp.full(slots.shape, -1.0, F32)
    peaks[...] = jnp.zeros_like(peaks)
    sigmas, ratios = [None] * mine, [None] * mine

    def own_q(index):
        sigmas[index] = multiply(bank.at[index], data_own, product.at[index % 2, 0])

    def own_d(index):
        inverse_long(product.at[index % 2, 0], back, twist_low, lines.at[index % 2], 0)

    def other_q(index):
        sigma_other = multiply(bank.at[index], data_other, product.at[index % 2, 1])
        ratios[index] = sigmas[index] / sigma_other

    def other_d(index):
        inverse_long(product.at[index % 2, 1], back, twist_low, lines.at[index % 2], 1)

    def both_sides(index, parities=(0, 1)):
        scale = 1.0 / (NFFT * sigmas[index])
        inverse_short(lines.at[index % 2], last, ratios[index], scale, peaks, 8 * index, parities)

    def multiplied(index):
        own_q(index)
        other_q(index)

    def inverted(index):
        own_d(index)
        other_d(index)

    multiplied(0)
    inverted(0)
    if mine > 1:
        multiplied(1)
    for index in range(mine):
        if index + 1 < mine:
            inverted(index + 1)
        if index + 2 < mine:
            multiplied(index + 2)
        both_sides(index)
    owners.wait()
    top = None
    for index, ordered in enumerate(in_block_order(peaks[...], order, mine)):
        top = ordered if top is None else jnp.maximum(top, ordered)
        here = detector * mine + index
        target = owner[here]
        rank = 0
        for other in range(per_dev):
            rank = rank + jnp.where(jnp.logical_and(owner[other] == target, other < here), 1, 0)
        slots[target, rank] = ordered
    rows = NBLK // BLK // n_det
    pad = send.shape[1] - rows * (capacity + 1)
    n_grp = send.shape[0] // (n_det * n_filt)
    for half in range(n_det):
        span = slice(half * rows, (half + 1) * rows)
        for place in range(n_filt):
            parts = [slots[place, rank, span] for rank in range(capacity)] + [top[span]]
            if pad:
                parts.append(jnp.full((pad, HALF), -1.0, F32))
            chunk = jnp.concatenate(parts, axis=0).astype(BF16)
            for group in range(n_grp):
                send[(half * n_grp + group) * n_filt + place] = chunk


def land_kernel(got, peaks_hbm, loudest_hbm, peaks, loudest, sems):
    n_det, n_grp, n_filt = lax.axis_size("det"), lax.axis_size("grp"), lax.axis_size("filt")
    group = lax.axis_index("grp")
    capacity = peaks.shape[0] // n_filt
    rows = peaks.shape[1] // BLK
    for place in range(n_filt):
        chunk = got[group * n_filt + place].astype(F32)
        for det in range(1, n_det):
            chunk = jnp.maximum(chunk, got[(det * n_grp + group) * n_filt + place].astype(F32))
        for rank in range(capacity):
            for part in range(rows):
                line = rank * rows + part
                peaks[pl.ds(place * capacity + rank, 1), pl.ds(part * BLK, BLK)] = chunk[line : line + 1]
    first = pltpu.make_async_copy(peaks, peaks_hbm, sems.at[0])
    first.start()
    top = got[0].astype(F32)
    for source in range(1, got.shape[0]):
        top = jnp.maximum(top, got[source].astype(F32))
    for part in range(rows):
        line = capacity * rows + part
        loudest[:, pl.ds(part * BLK, BLK)] = top[line : line + 1]
    second = pltpu.make_async_copy(loudest, loudest_hbm, sems.at[1])
    second.start()
    first.wait()
    second.wait()


def shards(tables, strain, inv_asd, templates, chirp_blocks, owner, slide):
    per_dev = templates.shape[0]
    n_det, n_grp, n_filt = lax.axis_size("det"), lax.axis_size("grp"), lax.axis_size("filt")
    mine = per_dev // n_det
    capacity = (per_dev + n_filt - 1) // n_filt
    swap = [(0, 1), (1, 0)]
    strain2d = strain.reshape(NBLK, BLK)
    weight_rows = inv_asd.reshape(NBLK // 2, BLK)
    vmem = pl.BlockSpec(memory_space=pltpu.VMEM)
    hbm = pl.BlockSpec(memory_space=pltpu.HBM)
    smem = pl.BlockSpec(memory_space=pltpu.SMEM)
    far = lambda value: pltpu.with_memory_space_constraint(value, pltpu.HBM)
    like = lambda value: pltpu.VMEM(value.shape, value.dtype)
    shape = jax.ShapeDtypeStruct
    params = pltpu.CompilerParams(vmem_limit_bytes=VMEM_LIMIT)
    twist_low, wide, tall = tables
    arrays = [templates, strain2d, weight_rows]
    data_own, bank_t, twist, twist_low, wide = pl.pallas_call(
        data_kernel,
        out_shape=[
            shape((3, N1, N1), BF16),
            shape((N2, ROWS * SLAB), BF16),
            shape(twist_low.shape, F32),
            shape(twist_low.shape, BF16),
            shape(wide.shape, BF16),
        ],
        in_specs=[smem] + [hbm] * 6,
        out_specs=[vmem] * 5,
        scratch_shapes=[pltpu.SMEM(chirp_blocks.shape, jnp.int32)]
        + [like(templates), like(weight_rows)]
        + [
            pltpu.VMEM((2 * NBLK, BLK), F32),
            pltpu.VMEM((N2, N1), BF16),
            pltpu.VMEM((2, N2, N1), BF16),
            pltpu.VMEM((ROWS * SLAB, N2), F32),
            pltpu.SemaphoreType.DMA((7,)),
        ],
        compiler_params=params,
        cost_estimate=pl.CostEstimate(flops=500_000_000, bytes_accessed=4_000_000, transcendentals=0),
        name="data_spectrum",
    )(slide, *[far(value) for value in (chirp_blocks, *arrays, twist_low, wide)])
    data_other = lax.ppermute(data_own, "det", swap)
    bank = pl.pallas_call(
        bank_kernel,
        out_shape=shape((mine, 2, N1, N1), BF16),
        in_specs=[vmem] * 3,
        out_specs=vmem,
        scratch_shapes=[pltpu.VMEM((2, 2, N2, N1), BF16)],
        compiler_params=params,
        cost_estimate=pl.CostEstimate(flops=2_000_000_000, bytes_accessed=4_000_000, transcendentals=0),
        name="bank_spectra",
    )(bank_t, twist, wide)

    half = NBLK // n_det
    rows = half // BLK
    depth = -(-rows * (capacity + 1) // 16) * 16
    everyone = n_det * n_grp * n_filt
    send = pl.pallas_call(
        filter_kernel,
        out_shape=shape((everyone, depth, BLK), BF16),
        in_specs=[hbm] + [vmem] * 5,
        out_specs=vmem,
        scratch_shapes=[
            pltpu.SMEM(owner.shape, jnp.int32),
            pltpu.VMEM((2, 2, 2, N1, N1), BF16),
            pltpu.VMEM((2, 2, 2 * N2, N1), BF16),
            pltpu.VMEM((HALF, HALF), F32),
            pltpu.VMEM((n_filt, capacity, 8, HALF), F32),
            pltpu.SemaphoreType.DMA,
        ],
        compiler_params=params,
        cost_estimate=pl.CostEstimate(flops=4_000_000_000, bytes_accessed=8_000_000, transcendentals=0),
        name="matched_filter",
    )(far(owner), bank, data_own, twist_low, tall, data_other)

    got = lax.all_to_all(send, ("det", "grp", "filt"), split_axis=0, concat_axis=0, tiled=True)
    slots = n_filt * capacity
    landed, loudest = pl.pallas_call(
        land_kernel,
        out_shape=[jax.ShapeDtypeStruct((slots, half), F32), jax.ShapeDtypeStruct((1, half), F32)],
        in_specs=[vmem],
        out_specs=[hbm, hbm],
        scratch_shapes=[pltpu.VMEM((slots, half), F32), pltpu.VMEM((1, half), F32), pltpu.SemaphoreType.DMA((2,))],
        compiler_params=pltpu.CompilerParams(vmem_limit_bytes=VMEM_LIMIT),
        name="land_peaks",
    )(got)
    loudest = loudest.reshape(half)
    if slots == per_dev:
        return landed, loudest
    positions = jnp.arange(per_dev, dtype=jnp.int32)
    valid = landed[:, 0] >= 0.0
    order = jnp.cumsum(valid.astype(jnp.int32)) - 1
    picker = jnp.logical_and(valid[None, :], order[None, :] == positions[:, None])
    return jnp.max(jnp.where(picker[:, :, None], landed[None], 0.0), axis=1), loudest


def solution(mesh):
    tables = make_tables()
    return jax.shard_map(
        functools.partial(shards, tables),
        mesh=mesh,
        in_specs=(
            P("det", None),
            P("det", None),
            P(("grp", "filt"), None),
            P(("grp", "filt")),
            P(("grp", "filt")),
            P("grp"),
        ),
        out_specs=(P(("grp", "filt"), "det"), P("det")),
        check_vma=False,
    )
```

```python
import functools

import jax
import jax.numpy as jnp
import ml_dtypes
import numpy as np
from jax import lax
from jax.experimental import pallas as pl
from jax.experimental.pallas import tpu as pltpu
from jax.sharding import PartitionSpec as P

N1 = 256
N2 = 512
NFFT = 131072
BLK = 128
NBLK = 1024
TL = 4096
ROWS = TL // N2
SLAB = 16
HALF = 128
CHUNK = 16
ORDER_BLOCKS = 3
BF16 = jnp.bfloat16
F32 = jnp.float32
VMEM_LIMIT = 16 * 1024 * 1024


def wave(left, right, period):
    angle = 2.0 * np.pi * ((np.asarray(left)[:, None] * np.asarray(right)[None, :]) % period) / period
    return np.cos(angle).astype(np.float32), np.sin(angle).astype(np.float32)


def make_tables():
    ar = np.arange
    cos_first, sin_first = wave(ar(N1), ar(N1), N1)
    first = np.concatenate([cos_first, -sin_first], axis=1)
    spread = np.repeat(first[:ROWS], SLAB, axis=0)
    cos_twist, sin_twist = wave(ar(N2), ar(N1), NFFT)
    ahead, back, last = [], [], []
    for parity in range(2):
        bins = 2 * ar(HALF) + parity
        cos_m, sin_m = wave(bins, ar(N1), N2)
        ahead.append(np.block([[cos_m, sin_m], [-sin_m, cos_m]]))
        pairs = np.block([[cos_m.T, -sin_m.T], [sin_m.T, cos_m.T]]).reshape(2, N1 // CHUNK, CHUNK, N1)
        back.append(pairs.transpose(1, 0, 2, 3).reshape(2 * N1, N1))
        cos_l, sin_l = wave(ar(HALF), bins, N1)
        last.append(np.block([[cos_l, sin_l], [-sin_l, cos_l]]))
    order = np.kron(np.eye(HALF // 8), np.tile(np.eye(8), (1, HALF // 8)))
    order = [order[:, start : start + N1] for start in range(0, order.shape[1], N1)]
    low = lambda parts: np.concatenate(parts).astype(ml_dtypes.bfloat16)
    return low([cos_twist, sin_twist]), low([spread] + ahead + [first]), low(back + last + order[:ORDER_BLOCKS])


def wide_parts(wide):
    return wide.at[pl.ds(0, HALF)], (wide.at[pl.ds(HALF, N1)], wide.at[pl.ds(HALF + N1, N1)]), wide.at[pl.ds(HALF + 2 * N1, N1)]


def tall_parts(tall):
    back = (tall.at[pl.ds(0, N2)], tall.at[pl.ds(N2, N2)])
    last = (tall.at[pl.ds(2 * N2, N1)], tall.at[pl.ds(2 * N2 + N1, N1)])
    return back, last, [tall.at[pl.ds(3 * N2 + index * HALF, HALF)] for index in range(ORDER_BLOCKS)]


def dot(left, right):
    return jnp.dot(left, right, preferred_element_type=F32)


def woven(index):
    halves = N1 // CHUNK
    return (2 * (index % halves) + index // halves) * CHUNK


def forward_first(signal, first, twist, folded, before_twist=None):
    both = dot(signal[...], first)
    if before_twist is not None:
        before_twist()
    for chunk in range(N1 // CHUNK):
        parts = []
        for half in range(2):
            base = (2 * chunk + half) * CHUNK
            real_a, imag_a = both[base : base + CHUNK, :N1], both[base : base + CHUNK, N1:]
            rows = pl.ds(half * N1 + chunk * CHUNK, CHUNK)
            cos_c, sin_c = twist[rows, :], twist[pl.ds(N2 + half * N1 + chunk * CHUNK, CHUNK), :]
            parts.append((real_a * cos_c + imag_a * sin_c, imag_a * cos_c - real_a * sin_c))
        (real_l, imag_l), (real_u, imag_u) = parts
        real, imag = pl.ds(chunk * CHUNK, CHUNK), pl.ds(N1 + chunk * CHUNK, CHUNK)
        folded[0, real, :] = (real_l + real_u).astype(BF16)
        folded[0, imag, :] = (imag_l + imag_u).astype(BF16)
        folded[1, real, :] = (real_l - real_u).astype(BF16)
        folded[1, imag, :] = (imag_l - imag_u).astype(BF16)


def forward_last(ahead, folded):
    return dot(ahead[0][...], folded[0]), dot(ahead[1][...], folded[1])


def data_spectrum(shift, weight, first, twist, ahead, twice, flipped, folded, data, before_twist):
    twice[pl.ds(NBLK, NBLK), :] = twice[pl.ds(0, NBLK), :]
    for part in range(N2 // BLK):
        block = twice[pl.ds(shift + part, N1, stride=N2 // BLK), :].astype(BF16).T
        for chunk in range(BLK // CHUNK):
            flipped[pl.ds(woven(part * (BLK // CHUNK) + chunk), CHUNK), :] = block[chunk * CHUNK : (chunk + 1) * CHUNK]
    forward_first(flipped, first[...], twist, folded, before_twist)
    halves = forward_last(ahead, folded)
    for parity in range(2):
        for part in range(2):
            lanes = slice(part * HALF, (part + 1) * HALF)
            kept = weight[pl.ds(2 * parity + part, HALF, stride=4), :]
            data[2, pl.ds(parity * HALF, HALF), lanes] = (kept * kept).astype(BF16)
            data[parity, :HALF, lanes] = (halves[parity][:HALF, lanes] * kept).astype(BF16)
            data[parity, HALF:, lanes] = (halves[parity][HALF:, lanes] * kept).astype(BF16)


def fetches(pairs, sems):
    return [pltpu.make_async_copy(source, target, sems.at[index]) for index, (source, target) in enumerate(pairs)]


def start_all(copies):
    for copy in copies:
        copy.start()


def wait_all(copies):
    for copy in copies:
        copy.wait()


def data_kernel(slide, blocks_hbm, templates_hbm, strain_hbm, weight_hbm, twist_low_hbm, wide_hbm,
                data, bank_t, twist, twist_low, wide,
                blocks, templates, weight, twice, flipped, folded, slabs, sems):
    total = templates.shape[0]
    detector = lax.axis_index("det")
    _, ahead, first = wide_parts(wide)
    copies = fetches(
        (
            (blocks_hbm, blocks),
            (templates_hbm, templates),
            (strain_hbm, twice.at[pl.ds(0, NBLK)]),
            (wide_hbm.at[pl.ds(HALF + 2 * N1, N1)], first),
            (wide_hbm.at[pl.ds(0, HALF + 2 * N1)], wide.at[pl.ds(0, HALF + 2 * N1)]),
            (twist_low_hbm, twist_low),
            (weight_hbm, weight),
        ),
        sems,
    )
    start_all(copies)

    def before_twist():
        copies[5].wait()
        twist[...] = twist_low[...].astype(F32)
        copies[4].wait()
        copies[6].wait()

    slabs[...] = jnp.zeros_like(slabs)
    row = lax.broadcasted_iota(jnp.int32, (total, N2), 0)
    column = lax.broadcasted_iota(jnp.int32, (total, N2), 1)
    wait_all(copies[:2])
    limit = jnp.zeros((total, N2), jnp.int32)
    for index in range(total):
        limit = jnp.where(row == index, BLK * blocks[index], limit)
    for part in range(ROWS):
        piece = templates[:, pl.ds(part * N2, N2)].astype(F32)
        slabs[pl.ds(part * SLAB, total), :] = jnp.where(column + part * N2 < limit, piece, 0.0)
    turned = slabs[...].astype(BF16).T
    for chunk in range(N2 // CHUNK):
        bank_t[pl.ds(woven(chunk), CHUNK), :] = turned[chunk * CHUNK : (chunk + 1) * CHUNK]
    wait_all(copies[2:4])
    shift = detector * slide[0]
    data_spectrum(shift, weight, first, twist, ahead, twice, flipped, folded, data, before_twist)


def bank_kernel(bank_t, twist, wide, bank, folded):
    mine = bank.shape[0]
    detector = lax.axis_index("det")
    spread, ahead, _ = wide_parts(wide)
    place = lax.broadcasted_iota(jnp.int32, spread.shape, 0) % SLAB

    def begin(index):
        picked = jnp.where(place == detector * mine + index, spread[...].astype(F32), 0.0).astype(BF16)
        forward_first(bank_t, picked, twist, folded.at[index % 2])

    begin(0)
    for index in range(mine):
        if index + 1 < mine:
            begin(index + 1)
        halves = forward_last(ahead, folded.at[index % 2])
        for parity in range(2):
            bank[index, parity] = halves[parity].astype(BF16)


def multiply(bank, sides, product):
    powers = [jnp.zeros((8, N1), F32) for _ in sides]
    for parity in range(2):
        pending = [None for _ in sides]
        for start in range(0, HALF, CHUNK):
            real, imag = pl.ds(start, CHUNK), pl.ds(HALF + start, CHUNK)
            bank_r, bank_i = bank[parity, real, :], bank[parity, imag, :]
            square = bank_r * bank_r + bank_i * bank_i
            for side, data in enumerate(sides):
                data_r, data_i = data[parity, real, :], data[parity, imag, :]
                each = data[2, pl.ds(parity * HALF + start, CHUNK), :] * square
                pending[side] = each if pending[side] is None else pending[side] + each
                if start // CHUNK % 2 == 1:
                    powers[side] = powers[side] + jnp.sum(pending[side].astype(F32).reshape(CHUNK // 8, 8, N1), axis=0)
                    pending[side] = None
                product[side, parity, real, :] = bank_r * data_r + bank_i * data_i
                product[side, parity, imag, :] = bank_r * data_i - bank_i * data_r
    return [jnp.sum(jnp.sum(power, axis=0, keepdims=True), axis=1, keepdims=True) for power in powers]


def inverse_long(product, back, twist, lines, side):
    even, odd = dot(back[0][...], product[0]), dot(back[1][...], product[1])
    for chunk in range(N1 // CHUNK):
        base = 2 * chunk * CHUNK
        real_e, imag_e = even[base : base + CHUNK], even[base + CHUNK : base + 2 * CHUNK]
        real_o, imag_o = odd[base : base + CHUNK], odd[base + CHUNK : base + 2 * CHUNK]
        real_e, imag_e, real_o, imag_o = [value.astype(BF16) for value in (real_e, imag_e, real_o, imag_o)]
        for place, real_d, imag_d in (
            (chunk, real_e + real_o, imag_e + imag_o),
            (chunk + N1 // CHUNK, real_e - real_o, imag_e - imag_o),
        ):
            cos_c, sin_c = twist[pl.ds(place * CHUNK, CHUNK), :], twist[pl.ds(N2 + place * CHUNK, CHUNK), :]
            real_w = real_d * cos_c - imag_d * sin_c
            imag_w = real_d * sin_c + imag_d * cos_c
            rows = pl.ds((2 * place + side) * CHUNK, CHUNK)
            lines[0, rows, :HALF] = real_w[:, :HALF] + real_w[:, HALF:]
            lines[0, rows, HALF:] = imag_w[:, :HALF] + imag_w[:, HALF:]
            lines[1, rows, :HALF] = real_w[:, :HALF] - real_w[:, HALF:]
            lines[1, rows, HALF:] = imag_w[:, :HALF] - imag_w[:, HALF:]


def inverse_short(lines, last, ratio, scale, peaks, base_row, parities=(0, 1)):
    for parity in parities:
        z = dot(lines[parity], last[parity][...])
        for part in range(N2 // BLK):
            best = None
            for chunk in range(BLK // CHUNK):
                base = 2 * (part * BLK + chunk * CHUNK)
                own, other = z[base : base + CHUNK], z[base + CHUNK : base + 2 * CHUNK]
                network = own[:, :HALF] * own[:, :HALF] + own[:, HALF:] * own[:, HALF:]
                network = network + (other[:, :HALF] * other[:, :HALF] + other[:, HALF:] * other[:, HALF:]) * ratio
                most = jnp.max(network.reshape(CHUNK // 8, 8, HALF), axis=0)
                best = most if best is None else jnp.maximum(best, most)
            peaks[pl.ds(base_row + 4 * parity + part, 1), :] = jnp.max(best, axis=0, keepdims=True) * scale


def in_block_order(peaks, order, mine):
    lane = lax.broadcasted_iota(jnp.int32, (HALF, HALF), 1)
    row = lax.broadcasted_iota(jnp.int32, (HALF, HALF), 0)
    turned = peaks.T.astype(BF16)
    result = []
    for index in range(mine):
        if index % 2 == 0:
            wide = dot(turned, order[index // 2][...])
        kept = jnp.where(lane // 8 == row % 16, wide[:, index % 2 * HALF : (index % 2 + 1) * HALF], 0.0)
        result.append(jnp.sum(kept.reshape(8, 16, HALF), axis=1))
    return result


def filter_kernel(owner_hbm, bank, data_own, twist_low, tall, data_other,
                  send,
                  owner, product, lines, peaks, slots, sem):
    mine, per_dev = bank.shape[0], owner.shape[0]
    n_filt, capacity = slots.shape[:2]
    n_det = per_dev // mine
    detector = lax.axis_index("det")
    back, last, order = tall_parts(tall)
    owners = pltpu.make_async_copy(owner_hbm, owner, sem)
    owners.start()
    slots[...] = jnp.full(slots.shape, -1.0, F32)
    peaks[...] = jnp.zeros_like(peaks)
    sigmas, ratios = [None] * mine, [None] * mine

    def own_d(index):
        inverse_long(product.at[index % 2, 0], back, twist_low, lines.at[index % 2], 0)

    def other_d(index):
        inverse_long(product.at[index % 2, 1], back, twist_low, lines.at[index % 2], 1)

    def both_sides(index, parities=(0, 1)):
        scale = 1.0 / (NFFT * sigmas[index])
        inverse_short(lines.at[index % 2], last, ratios[index], scale, peaks, 8 * index, parities)

    def multiplied(index):
        own, other = multiply(bank.at[index], (data_own, data_other), product.at[index % 2])
        sigmas[index], ratios[index] = own, own / other

    def inverted(index):
        own_d(index)
        other_d(index)

    multiplied(0)
    inverted(0)
    if mine > 1:
        multiplied(1)
    for index in range(mine):
        if index + 1 < mine:
            inverted(index + 1)
        if index + 2 < mine:
            multiplied(index + 2)
        both_sides(index)
    owners.wait()
    top = None
    for index, ordered in enumerate(in_block_order(peaks[...], order, mine)):
        top = ordered if top is None else jnp.maximum(top, ordered)
        here = detector * mine + index
        target = owner[here]
        rank = 0
        for other in range(per_dev):
            rank = rank + jnp.where(jnp.logical_and(owner[other] == target, other < here), 1, 0)
        slots[target, rank] = ordered
    rows = NBLK // BLK // n_det
    pad = send.shape[1] - rows * (capacity + 1)
    n_grp = send.shape[0] // (n_det * n_filt)
    for half in range(n_det):
        span = slice(half * rows, (half + 1) * rows)
        for place in range(n_filt):
            parts = [slots[place, rank, span] for rank in range(capacity)] + [top[span]]
            if pad:
                parts.append(jnp.full((pad, HALF), -1.0, F32))
            chunk = jnp.concatenate(parts, axis=0).astype(BF16)
            for group in range(n_grp):
                send[(half * n_grp + group) * n_filt + place] = chunk


def land_kernel(got, peaks_hbm, loudest_hbm, peaks, loudest, sems):
    n_det, n_grp, n_filt = lax.axis_size("det"), lax.axis_size("grp"), lax.axis_size("filt")
    group = lax.axis_index("grp")
    capacity = peaks.shape[0] // n_filt
    rows = peaks.shape[1] // BLK
    for place in range(n_filt):
        chunk = got[group * n_filt + place].astype(F32)
        for det in range(1, n_det):
            chunk = jnp.maximum(chunk, got[(det * n_grp + group) * n_filt + place].astype(F32))
        for rank in range(capacity):
            for part in range(rows):
                line = rank * rows + part
                peaks[pl.ds(place * capacity + rank, 1), pl.ds(part * BLK, BLK)] = chunk[line : line + 1]
    first = pltpu.make_async_copy(peaks, peaks_hbm, sems.at[0])
    first.start()
    top = got[0].astype(F32)
    for source in range(1, got.shape[0]):
        top = jnp.maximum(top, got[source].astype(F32))
    for part in range(rows):
        line = capacity * rows + part
        loudest[:, pl.ds(part * BLK, BLK)] = top[line : line + 1]
    second = pltpu.make_async_copy(loudest, loudest_hbm, sems.at[1])
    second.start()
    first.wait()
    second.wait()


def shards(tables, strain, inv_asd, templates, chirp_blocks, owner, slide):
    per_dev = templates.shape[0]
    n_det, n_grp, n_filt = lax.axis_size("det"), lax.axis_size("grp"), lax.axis_size("filt")
    mine = per_dev // n_det
    capacity = (per_dev + n_filt - 1) // n_filt
    swap = [(0, 1), (1, 0)]
    strain2d = strain.reshape(NBLK, BLK)
    weight_rows = inv_asd.reshape(NBLK // 2, BLK)
    vmem = pl.BlockSpec(memory_space=pltpu.VMEM)
    hbm = pl.BlockSpec(memory_space=pltpu.HBM)
    smem = pl.BlockSpec(memory_space=pltpu.SMEM)
    far = lambda value: pltpu.with_memory_space_constraint(value, pltpu.HBM)
    like = lambda value: pltpu.VMEM(value.shape, value.dtype)
    shape = jax.ShapeDtypeStruct
    params = pltpu.CompilerParams(vmem_limit_bytes=VMEM_LIMIT)
    twist_low, wide, tall = tables
    arrays = [templates, strain2d, weight_rows]
    data_own, bank_t, twist, twist_low, wide = pl.pallas_call(
        data_kernel,
        out_shape=[
            shape((3, N1, N1), BF16),
            shape((N2, ROWS * SLAB), BF16),
            shape(twist_low.shape, F32),
            shape(twist_low.shape, BF16),
            shape(wide.shape, BF16),
        ],
        in_specs=[smem] + [hbm] * 6,
        out_specs=[vmem] * 5,
        scratch_shapes=[pltpu.SMEM(chirp_blocks.shape, jnp.int32)]
        + [like(templates), like(weight_rows)]
        + [
            pltpu.VMEM((2 * NBLK, BLK), F32),
            pltpu.VMEM((N2, N1), BF16),
            pltpu.VMEM((2, N2, N1), BF16),
            pltpu.VMEM((ROWS * SLAB, N2), F32),
            pltpu.SemaphoreType.DMA((7,)),
        ],
        compiler_params=params,
        cost_estimate=pl.CostEstimate(flops=500_000_000, bytes_accessed=4_000_000, transcendentals=0),
        name="data_spectrum",
    )(slide, *[far(value) for value in (chirp_blocks, *arrays, twist_low, wide)])
    data_other = lax.ppermute(data_own, "det", swap)
    bank = pl.pallas_call(
        bank_kernel,
        out_shape=shape((mine, 2, N1, N1), BF16),
        in_specs=[vmem] * 3,
        out_specs=vmem,
        scratch_shapes=[pltpu.VMEM((2, 2, N2, N1), BF16)],
        compiler_params=params,
        cost_estimate=pl.CostEstimate(flops=2_000_000_000, bytes_accessed=4_000_000, transcendentals=0),
        name="bank_spectra",
    )(bank_t, twist, wide)

    half = NBLK // n_det
    rows = half // BLK
    depth = -(-rows * (capacity + 1) // 16) * 16
    everyone = n_det * n_grp * n_filt
    send = pl.pallas_call(
        filter_kernel,
        out_shape=shape((everyone, depth, BLK), BF16),
        in_specs=[hbm] + [vmem] * 5,
        out_specs=vmem,
        scratch_shapes=[
            pltpu.SMEM(owner.shape, jnp.int32),
            pltpu.VMEM((2, 2, 2, N1, N1), BF16),
            pltpu.VMEM((2, 2, 2 * N2, N1), BF16),
            pltpu.VMEM((HALF, HALF), F32),
            pltpu.VMEM((n_filt, capacity, 8, HALF), F32),
            pltpu.SemaphoreType.DMA,
        ],
        compiler_params=params,
        cost_estimate=pl.CostEstimate(flops=4_000_000_000, bytes_accessed=8_000_000, transcendentals=0),
        name="matched_filter",
    )(far(owner), bank, data_own, twist_low, tall, data_other)

    got = lax.all_to_all(send, ("det", "grp", "filt"), split_axis=0, concat_axis=0, tiled=True)
    slots = n_filt * capacity
    landed, loudest = pl.pallas_call(
        land_kernel,
        out_shape=[jax.ShapeDtypeStruct((slots, half), F32), jax.ShapeDtypeStruct((1, half), F32)],
        in_specs=[vmem],
        out_specs=[hbm, hbm],
        scratch_shapes=[pltpu.VMEM((slots, half), F32), pltpu.VMEM((1, half), F32), pltpu.SemaphoreType.DMA((2,))],
        compiler_params=pltpu.CompilerParams(vmem_limit_bytes=VMEM_LIMIT),
        name="land_peaks",
    )(got)
    loudest = loudest.reshape(half)
    if slots == per_dev:
        return landed, loudest
    positions = jnp.arange(per_dev, dtype=jnp.int32)
    valid = landed[:, 0] >= 0.0
    order = jnp.cumsum(valid.astype(jnp.int32)) - 1
    picker = jnp.logical_and(valid[None, :], order[None, :] == positions[:, None])
    return jnp.max(jnp.where(picker[:, :, None], landed[None], 0.0), axis=1), loudest


def solution(mesh):
    tables = make_tables()
    return jax.shard_map(
        functools.partial(shards, tables),
        mesh=mesh,
        in_specs=(
            P("det", None),
            P("det", None),
            P(("grp", "filt"), None),
            P(("grp", "filt")),
            P(("grp", "filt")),
            P("grp"),
        ),
        out_specs=(P(("grp", "filt"), "det"), P("det")),
        check_vma=False,
    )
```

```python
import functools

import jax
import jax.numpy as jnp
import ml_dtypes
import numpy as np
from jax import lax
from jax.experimental import pallas as pl
from jax.experimental.pallas import tpu as pltpu
from jax.sharding import PartitionSpec as P

N1 = 256
N2 = 512
NFFT = 131072
BLK = 128
NBLK = 1024
TL = 4096
ROWS = TL // N2
SLAB = 16
HALF = 128
CHUNK = 16
ORDER_BLOCKS = 3
BF16 = jnp.bfloat16
F32 = jnp.float32
VMEM_LIMIT = 16 * 1024 * 1024


def wave(left, right, period):
    angle = 2.0 * np.pi * ((np.asarray(left)[:, None] * np.asarray(right)[None, :]) % period) / period
    return np.cos(angle).astype(np.float32), np.sin(angle).astype(np.float32)


def make_tables():
    ar = np.arange
    cos_first, sin_first = wave(ar(N1), ar(N1), N1)
    first = np.concatenate([cos_first, -sin_first], axis=1)
    spread = np.repeat(first[:ROWS], SLAB, axis=0)
    cos_twist, sin_twist = wave(ar(N2), ar(N1), NFFT)
    ahead, back, last = [], [], []
    for parity in range(2):
        bins = 2 * ar(HALF) + parity
        cos_m, sin_m = wave(bins, ar(N1), N2)
        ahead.append(np.block([[cos_m, sin_m], [-sin_m, cos_m]]))
        pairs = np.block([[cos_m.T, -sin_m.T], [sin_m.T, cos_m.T]]).reshape(2, N1 // CHUNK, CHUNK, N1)
        back.append(pairs.transpose(1, 0, 2, 3).reshape(2 * N1, N1))
        cos_l, sin_l = wave(ar(HALF), bins, N1)
        last.append(np.block([[cos_l, sin_l], [-sin_l, cos_l]]))
    order = np.kron(np.eye(HALF // 8), np.tile(np.eye(8), (1, HALF // 8)))
    order = [order[:, start : start + N1] for start in range(0, order.shape[1], N1)]
    low = lambda parts: np.concatenate(parts).astype(ml_dtypes.bfloat16)
    return low([cos_twist, sin_twist]), low([spread] + ahead + [first]), low(back + last + order[:ORDER_BLOCKS])


def wide_parts(wide):
    return wide.at[pl.ds(0, HALF)], (wide.at[pl.ds(HALF, N1)], wide.at[pl.ds(HALF + N1, N1)]), wide.at[pl.ds(HALF + 2 * N1, N1)]


def tall_parts(tall):
    back = (tall.at[pl.ds(0, N2)], tall.at[pl.ds(N2, N2)])
    last = (tall.at[pl.ds(2 * N2, N1)], tall.at[pl.ds(2 * N2 + N1, N1)])
    return back, last, [tall.at[pl.ds(3 * N2 + index * HALF, HALF)] for index in range(ORDER_BLOCKS)]


def dot(left, right):
    return jnp.dot(left, right, preferred_element_type=F32)


def woven(index):
    halves = N1 // CHUNK
    return (2 * (index % halves) + index // halves) * CHUNK


def forward_first(signal, first, twist, folded, before_twist=None):
    both = dot(signal[...], first)
    if before_twist is not None:
        before_twist()
    for chunk in range(N1 // CHUNK):
        parts = []
        for half in range(2):
            base = (2 * chunk + half) * CHUNK
            real_a, imag_a = both[base : base + CHUNK, :N1], both[base : base + CHUNK, N1:]
            rows = pl.ds(half * N1 + chunk * CHUNK, CHUNK)
            cos_c, sin_c = twist[rows, :], twist[pl.ds(N2 + half * N1 + chunk * CHUNK, CHUNK), :]
            parts.append((real_a * cos_c + imag_a * sin_c, imag_a * cos_c - real_a * sin_c))
        (real_l, imag_l), (real_u, imag_u) = parts
        real, imag = pl.ds(chunk * CHUNK, CHUNK), pl.ds(N1 + chunk * CHUNK, CHUNK)
        folded[0, real, :] = (real_l + real_u).astype(BF16)
        folded[0, imag, :] = (imag_l + imag_u).astype(BF16)
        folded[1, real, :] = (real_l - real_u).astype(BF16)
        folded[1, imag, :] = (imag_l - imag_u).astype(BF16)


def forward_last(ahead, folded):
    return dot(ahead[0][...], folded[0]), dot(ahead[1][...], folded[1])


def data_spectrum(shift, weight, first, twist, ahead, twice, flipped, folded, data, before_twist, before_ahead):
    twice[pl.ds(NBLK, NBLK), :] = twice[pl.ds(0, NBLK), :]
    for part in range(N2 // BLK):
        block = twice[pl.ds(shift + part, N1, stride=N2 // BLK), :].astype(BF16).T
        for chunk in range(BLK // CHUNK):
            flipped[pl.ds(woven(part * (BLK // CHUNK) + chunk), CHUNK), :] = block[chunk * CHUNK : (chunk + 1) * CHUNK]
    forward_first(flipped, first[...], twist, folded, before_twist)
    before_ahead()
    halves = forward_last(ahead, folded)
    for parity in range(2):
        for part in range(2):
            lanes = slice(part * HALF, (part + 1) * HALF)
            kept = weight[pl.ds(2 * parity + part, HALF, stride=4), :]
            data[2, pl.ds(parity * HALF, HALF), lanes] = (kept * kept).astype(BF16)
            data[parity, :HALF, lanes] = (halves[parity][:HALF, lanes] * kept).astype(BF16)
            data[parity, HALF:, lanes] = (halves[parity][HALF:, lanes] * kept).astype(BF16)


def fetches(pairs, sems):
    return [pltpu.make_async_copy(source, target, sems.at[index]) for index, (source, target) in enumerate(pairs)]


def start_all(copies):
    for copy in copies:
        copy.start()


def wait_all(copies):
    for copy in copies:
        copy.wait()


def data_kernel(slide, blocks_hbm, templates_hbm, strain_hbm, weight_hbm, twist_low_hbm, wide_hbm,
                data, bank_t, twist, twist_low, wide,
                blocks, templates, weight, twice, flipped, folded, slabs, sems):
    total = templates.shape[0]
    detector = lax.axis_index("det")
    _, ahead, first = wide_parts(wide)
    copies = fetches(
        (
            (blocks_hbm, blocks),
            (templates_hbm, templates),
            (strain_hbm, twice.at[pl.ds(0, NBLK)]),
            (wide_hbm.at[pl.ds(HALF + 2 * N1, N1)], first),
            (twist_low_hbm, twist_low),
            (wide_hbm.at[pl.ds(0, HALF + 2 * N1)], wide.at[pl.ds(0, HALF + 2 * N1)]),
            (weight_hbm, weight),
        ),
        sems,
    )
    start_all(copies)

    def before_twist():
        copies[4].wait()
        twist[...] = twist_low[...].astype(F32)

    def before_ahead():
        wait_all(copies[5:7])

    slabs[...] = jnp.zeros_like(slabs)
    row = lax.broadcasted_iota(jnp.int32, (total, N2), 0)
    column = lax.broadcasted_iota(jnp.int32, (total, N2), 1)
    wait_all(copies[:2])
    limit = jnp.zeros((total, N2), jnp.int32)
    for index in range(total):
        limit = jnp.where(row == index, BLK * blocks[index], limit)
    for part in range(ROWS):
        piece = templates[:, pl.ds(part * N2, N2)].astype(F32)
        slabs[pl.ds(part * SLAB, total), :] = jnp.where(column + part * N2 < limit, piece, 0.0)
    turned = slabs[...].astype(BF16).T
    for chunk in range(N2 // CHUNK):
        bank_t[pl.ds(woven(chunk), CHUNK), :] = turned[chunk * CHUNK : (chunk + 1) * CHUNK]
    wait_all(copies[2:4])
    shift = detector * slide[0]
    data_spectrum(shift, weight, first, twist, ahead, twice, flipped, folded, data, before_twist, before_ahead)


def bank_kernel(bank_t, twist, wide, bank, folded):
    mine = bank.shape[0]
    detector = lax.axis_index("det")
    spread, ahead, _ = wide_parts(wide)
    place = lax.broadcasted_iota(jnp.int32, spread.shape, 0) % SLAB

    def begin(index):
        picked = jnp.where(place == detector * mine + index, spread[...].astype(F32), 0.0).astype(BF16)
        forward_first(bank_t, picked, twist, folded.at[index % 2])

    begin(0)
    for index in range(mine):
        if index + 1 < mine:
            begin(index + 1)
        halves = forward_last(ahead, folded.at[index % 2])
        for parity in range(2):
            bank[index, parity] = halves[parity].astype(BF16)


def multiply(bank, sides, product):
    powers = [jnp.zeros((8, N1), F32) for _ in sides]
    for parity in range(2):
        pending = [None for _ in sides]
        for start in range(0, HALF, CHUNK):
            real, imag = pl.ds(start, CHUNK), pl.ds(HALF + start, CHUNK)
            bank_r, bank_i = bank[parity, real, :], bank[parity, imag, :]
            square = bank_r * bank_r + bank_i * bank_i
            for side, data in enumerate(sides):
                data_r, data_i = data[parity, real, :], data[parity, imag, :]
                each = data[2, pl.ds(parity * HALF + start, CHUNK), :] * square
                pending[side] = each if pending[side] is None else pending[side] + each
                if start // CHUNK % 2 == 1:
                    powers[side] = powers[side] + jnp.sum(pending[side].astype(F32).reshape(CHUNK // 8, 8, N1), axis=0)
                    pending[side] = None
                product[side, parity, real, :] = bank_r * data_r + bank_i * data_i
                product[side, parity, imag, :] = bank_r * data_i - bank_i * data_r
    return [jnp.sum(jnp.sum(power, axis=0, keepdims=True), axis=1, keepdims=True) for power in powers]


def inverse_long(product, back, twist, lines, side):
    even, odd = dot(back[0][...], product[0]), dot(back[1][...], product[1])
    for chunk in range(N1 // CHUNK):
        base = 2 * chunk * CHUNK
        real_e, imag_e = even[base : base + CHUNK], even[base + CHUNK : base + 2 * CHUNK]
        real_o, imag_o = odd[base : base + CHUNK], odd[base + CHUNK : base + 2 * CHUNK]
        real_e, imag_e, real_o, imag_o = [value.astype(BF16) for value in (real_e, imag_e, real_o, imag_o)]
        for place, real_d, imag_d in (
            (chunk, real_e + real_o, imag_e + imag_o),
            (chunk + N1 // CHUNK, real_e - real_o, imag_e - imag_o),
        ):
            cos_c, sin_c = twist[pl.ds(place * CHUNK, CHUNK), :], twist[pl.ds(N2 + place * CHUNK, CHUNK), :]
            real_w = real_d * cos_c - imag_d * sin_c
            imag_w = real_d * sin_c + imag_d * cos_c
            rows = pl.ds((2 * place + side) * CHUNK, CHUNK)
            lines[0, rows, :HALF] = real_w[:, :HALF] + real_w[:, HALF:]
            lines[0, rows, HALF:] = imag_w[:, :HALF] + imag_w[:, HALF:]
            lines[1, rows, :HALF] = real_w[:, :HALF] - real_w[:, HALF:]
            lines[1, rows, HALF:] = imag_w[:, :HALF] - imag_w[:, HALF:]


def inverse_short(lines, last, ratio, scale, peaks, base_row, parities=(0, 1)):
    for parity in parities:
        z = dot(lines[parity], last[parity][...])
        for part in range(N2 // BLK):
            best = None
            for chunk in range(BLK // CHUNK):
                base = 2 * (part * BLK + chunk * CHUNK)
                own, other = z[base : base + CHUNK], z[base + CHUNK : base + 2 * CHUNK]
                network = own[:, :HALF] * own[:, :HALF] + own[:, HALF:] * own[:, HALF:]
                network = network + (other[:, :HALF] * other[:, :HALF] + other[:, HALF:] * other[:, HALF:]) * ratio
                most = jnp.max(network.reshape(CHUNK // 8, 8, HALF), axis=0)
                best = most if best is None else jnp.maximum(best, most)
            peaks[pl.ds(base_row + 4 * parity + part, 1), :] = jnp.max(best, axis=0, keepdims=True) * scale


def in_block_order(peaks, order, mine):
    lane = lax.broadcasted_iota(jnp.int32, (HALF, HALF), 1)
    row = lax.broadcasted_iota(jnp.int32, (HALF, HALF), 0)
    turned = peaks.T.astype(BF16)
    result = []
    for index in range(mine):
        if index % 2 == 0:
            wide = dot(turned, order[index // 2][...])
        kept = jnp.where(lane // 8 == row % 16, wide[:, index % 2 * HALF : (index % 2 + 1) * HALF], 0.0)
        result.append(jnp.sum(kept.reshape(8, 16, HALF), axis=1))
    return result


def filter_kernel(owner_hbm, bank, data_own, twist_low, tall, data_other,
                  send,
                  owner, product, lines, peaks, slots, sem):
    mine, per_dev = bank.shape[0], owner.shape[0]
    n_filt, capacity = slots.shape[:2]
    n_det = per_dev // mine
    detector = lax.axis_index("det")
    back, last, order = tall_parts(tall)
    owners = pltpu.make_async_copy(owner_hbm, owner, sem)
    owners.start()
    slots[...] = jnp.full(slots.shape, -1.0, F32)
    peaks[...] = jnp.zeros_like(peaks)
    sigmas, ratios = [None] * mine, [None] * mine

    def own_d(index):
        inverse_long(product.at[index % 2, 0], back, twist_low, lines.at[index % 2], 0)

    def other_d(index):
        inverse_long(product.at[index % 2, 1], back, twist_low, lines.at[index % 2], 1)

    def both_sides(index, parities=(0, 1)):
        scale = 1.0 / (NFFT * sigmas[index])
        inverse_short(lines.at[index % 2], last, ratios[index], scale, peaks, 8 * index, parities)

    def multiplied(index):
        own, other = multiply(bank.at[index], (data_own, data_other), product.at[index % 2])
        sigmas[index], ratios[index] = own, own / other

    def inverted(index):
        own_d(index)
        other_d(index)

    multiplied(0)
    inverted(0)
    if mine > 1:
        multiplied(1)
    for index in range(mine):
        if index + 1 < mine:
            inverted(index + 1)
        if index + 2 < mine:
            multiplied(index + 2)
        both_sides(index)
    owners.wait()
    top = None
    for index, ordered in enumerate(in_block_order(peaks[...], order, mine)):
        top = ordered if top is None else jnp.maximum(top, ordered)
        here = detector * mine + index
        target = owner[here]
        rank = 0
        for other in range(per_dev):
            rank = rank + jnp.where(jnp.logical_and(owner[other] == target, other < here), 1, 0)
        slots[target, rank] = ordered
    rows = NBLK // BLK // n_det
    pad = send.shape[1] - rows * (capacity + 1)
    n_grp = send.shape[0] // (n_det * n_filt)
    for half in range(n_det):
        span = slice(half * rows, (half + 1) * rows)
        for place in range(n_filt):
            parts = [slots[place, rank, span] for rank in range(capacity)] + [top[span]]
            if pad:
                parts.append(jnp.full((pad, HALF), -1.0, F32))
            chunk = jnp.concatenate(parts, axis=0).astype(BF16)
            for group in range(n_grp):
                send[(half * n_grp + group) * n_filt + place] = chunk


def land_kernel(got, peaks_hbm, loudest_hbm, peaks, loudest, sems):
    n_det, n_grp, n_filt = lax.axis_size("det"), lax.axis_size("grp"), lax.axis_size("filt")
    group = lax.axis_index("grp")
    capacity = peaks.shape[0] // n_filt
    rows = peaks.shape[1] // BLK
    for place in range(n_filt):
        chunk = got[group * n_filt + place].astype(F32)
        for det in range(1, n_det):
            chunk = jnp.maximum(chunk, got[(det * n_grp + group) * n_filt + place].astype(F32))
        for rank in range(capacity):
            for part in range(rows):
                line = rank * rows + part
                peaks[pl.ds(place * capacity + rank, 1), pl.ds(part * BLK, BLK)] = chunk[line : line + 1]
    first = pltpu.make_async_copy(peaks, peaks_hbm, sems.at[0])
    first.start()
    top = got[0].astype(F32)
    for source in range(1, got.shape[0]):
        top = jnp.maximum(top, got[source].astype(F32))
    for part in range(rows):
        line = capacity * rows + part
        loudest[:, pl.ds(part * BLK, BLK)] = top[line : line + 1]
    second = pltpu.make_async_copy(loudest, loudest_hbm, sems.at[1])
    second.start()
    first.wait()
    second.wait()


def shards(tables, strain, inv_asd, templates, chirp_blocks, owner, slide):
    per_dev = templates.shape[0]
    n_det, n_grp, n_filt = lax.axis_size("det"), lax.axis_size("grp"), lax.axis_size("filt")
    mine = per_dev // n_det
    capacity = (per_dev + n_filt - 1) // n_filt
    swap = [(0, 1), (1, 0)]
    strain2d = strain.reshape(NBLK, BLK)
    weight_rows = inv_asd.reshape(NBLK // 2, BLK)
    vmem = pl.BlockSpec(memory_space=pltpu.VMEM)
    hbm = pl.BlockSpec(memory_space=pltpu.HBM)
    smem = pl.BlockSpec(memory_space=pltpu.SMEM)
    far = lambda value: pltpu.with_memory_space_constraint(value, pltpu.HBM)
    like = lambda value: pltpu.VMEM(value.shape, value.dtype)
    shape = jax.ShapeDtypeStruct
    params = pltpu.CompilerParams(vmem_limit_bytes=VMEM_LIMIT)
    twist_low, wide, tall = tables
    arrays = [templates, strain2d, weight_rows]
    data_own, bank_t, twist, twist_low, wide = pl.pallas_call(
        data_kernel,
        out_shape=[
            shape((3, N1, N1), BF16),
            shape((N2, ROWS * SLAB), BF16),
            shape(twist_low.shape, F32),
            shape(twist_low.shape, BF16),
            shape(wide.shape, BF16),
        ],
        in_specs=[smem] + [hbm] * 6,
        out_specs=[vmem] * 5,
        scratch_shapes=[pltpu.SMEM(chirp_blocks.shape, jnp.int32)]
        + [like(templates), like(weight_rows)]
        + [
            pltpu.VMEM((2 * NBLK, BLK), F32),
            pltpu.VMEM((N2, N1), BF16),
            pltpu.VMEM((2, N2, N1), BF16),
            pltpu.VMEM((ROWS * SLAB, N2), F32),
            pltpu.SemaphoreType.DMA((7,)),
        ],
        compiler_params=params,
        cost_estimate=pl.CostEstimate(flops=500_000_000, bytes_accessed=4_000_000, transcendentals=0),
        name="data_spectrum",
    )(slide, *[far(value) for value in (chirp_blocks, *arrays, twist_low, wide)])
    data_other = lax.ppermute(data_own, "det", swap)
    bank = pl.pallas_call(
        bank_kernel,
        out_shape=shape((mine, 2, N1, N1), BF16),
        in_specs=[vmem] * 3,
        out_specs=vmem,
        scratch_shapes=[pltpu.VMEM((2, 2, N2, N1), BF16)],
        compiler_params=params,
        cost_estimate=pl.CostEstimate(flops=2_000_000_000, bytes_accessed=4_000_000, transcendentals=0),
        name="bank_spectra",
    )(bank_t, twist, wide)

    half = NBLK // n_det
    rows = half // BLK
    depth = -(-rows * (capacity + 1) // 16) * 16
    everyone = n_det * n_grp * n_filt
    send = pl.pallas_call(
        filter_kernel,
        out_shape=shape((everyone, depth, BLK), BF16),
        in_specs=[hbm] + [vmem] * 5,
        out_specs=vmem,
        scratch_shapes=[
            pltpu.SMEM(owner.shape, jnp.int32),
            pltpu.VMEM((2, 2, 2, N1, N1), BF16),
            pltpu.VMEM((2, 2, 2 * N2, N1), BF16),
            pltpu.VMEM((HALF, HALF), F32),
            pltpu.VMEM((n_filt, capacity, 8, HALF), F32),
            pltpu.SemaphoreType.DMA,
        ],
        compiler_params=params,
        cost_estimate=pl.CostEstimate(flops=4_000_000_000, bytes_accessed=8_000_000, transcendentals=0),
        name="matched_filter",
    )(far(owner), bank, data_own, twist_low, tall, data_other)

    got = lax.all_to_all(send, ("det", "grp", "filt"), split_axis=0, concat_axis=0, tiled=True)
    slots = n_filt * capacity
    landed, loudest = pl.pallas_call(
        land_kernel,
        out_shape=[jax.ShapeDtypeStruct((slots, half), F32), jax.ShapeDtypeStruct((1, half), F32)],
        in_specs=[vmem],
        out_specs=[hbm, hbm],
        scratch_shapes=[pltpu.VMEM((slots, half), F32), pltpu.VMEM((1, half), F32), pltpu.SemaphoreType.DMA((2,))],
        compiler_params=pltpu.CompilerParams(vmem_limit_bytes=VMEM_LIMIT),
        name="land_peaks",
    )(got)
    loudest = loudest.reshape(half)
    if slots == per_dev:
        return landed, loudest
    positions = jnp.arange(per_dev, dtype=jnp.int32)
    valid = landed[:, 0] >= 0.0
    order = jnp.cumsum(valid.astype(jnp.int32)) - 1
    picker = jnp.logical_and(valid[None, :], order[None, :] == positions[:, None])
    return jnp.max(jnp.where(picker[:, :, None], landed[None], 0.0), axis=1), loudest


def solution(mesh):
    tables = make_tables()
    return jax.shard_map(
        functools.partial(shards, tables),
        mesh=mesh,
        in_specs=(
            P("det", None),
            P("det", None),
            P(("grp", "filt"), None),
            P(("grp", "filt")),
            P(("grp", "filt")),
            P("grp"),
        ),
        out_specs=(P(("grp", "filt"), "det"), P("det")),
        check_vma=False,
    )
```
